32 devices in a mesh: section: 2 (over x), dp: 4 (over z), tensor: 4 (over y, core).
Axes of the slice: x: 2, y: 2, z: 4, core: 2. Of those that a mesh axis runs over, the one named last changes fastest.
Arguments:
- layer_input: bfloat16 [4, 3328, 768], P(None, ('dp', 'tensor')), may hold values from -6 to 6
- cotangent: bfloat16 [4, 3328, 768], P(None, ('dp', 'tensor')), may hold values from -6 to 6
- region_count: int32 [4, 16], P(None, 'dp'), may hold values from 10 to 80
- region_mask: int32 [4, 16, 80], P(None, 'dp'), may hold values 0 or 1
- attn_weight: bfloat16 [2, 768, 12, 192], P('section', None, 'tensor'), may hold values from -0.21875 to 0.21875
- attn_bias: float32 [2, 12, 128], P('section', 'tensor'), may hold values from -0.6 to 0.6
- proj_weight: bfloat16 [2, 12, 64, 768], P('section', 'tensor'), may hold values from -1.5 to 1.5
- proj_bias: float32 [2, 768], P('section'), may hold values from -1.8 to 1.8
- first_gain: float32 [2, 768], P('section'), may hold values from 0.5 to 1.5
- first_shift: float32 [2, 768], P('section'), may hold values from -1.8 to 1.8
- up_weight: bfloat16 [2, 768, 3072], P('section', None, 'tensor'), may hold values from -0.21875 to 0.21875
- up_bias: float32 [2, 3072], P('section', 'tensor'), may hold values from -1.8 to 1.8
- down_weight: bfloat16 [2, 3072, 768], P('section', 'tensor'), may hold values from -0.109375 to 0.109375
- down_bias: float32 [2, 768], P('section'), may hold values from -1.8 to 1.8
- second_gain: float32 [2, 768], P('section'), may hold values from 0.5 to 1.5
- second_shift: float32 [2, 768], P('section'), may hold values from -1.8 to 1.8
Outputs:
- layer_outputs: bfloat16 [2, 4, 3328, 768], P('section', None, ('dp', 'tensor'))
- input_grads: float32 [2, 4, 3328, 768], P('section', None, ('dp', 'tensor'))
- grad_attn_weight: float32 [2, 768, 12, 192], P('section', None, 'tensor')
- grad_attn_bias: float32 [2, 12, 128], P('section', 'tensor')
- grad_proj_weight: float32 [2, 12, 64, 768], P('section', 'tensor')
- grad_proj_bias: float32 [2, 768], P('section')
- grad_first_gain: float32 [2, 768], P('section')
- grad_first_shift: float32 [2, 768], P('section')
- grad_up_weight: float32 [2, 768, 3072], P('section', None, 'tensor')
- grad_up_bias: float32 [2, 3072], P('section', 'tensor')
- grad_down_weight: float32 [2, 3072, 768], P('section', 'tensor')
- grad_down_bias: float32 [2, 768], P('section')
- grad_second_gain: float32 [2, 768], P('section')
- grad_second_shift: float32 [2, 768], P('section')
The draws below stay inside these ranges and needn't reach their ends.
Inputs may be any that keep to these rules, and one draw needn't show every extreme that they name: `region_mask`: 1 marks a usable region slot.
All inputs are finite; a program needn't handle non-finite values. No bound on the sum of `region_mask` on one device may be relied on, other than what follows from the above.
Results may differ from the reference program's by a relative error of at most 0.025.
Values may be sent and summed in bfloat16 or wider, within the bound.
No kernel may reach another device: no remote copies, remote signals or barrier semaphores. Data moves between devices by JAX's collectives and lax.ppermute only.
A program may use at most 192 MiB of HBM per device.

```python
import jax
import jax.numpy as jnp
from jax import lax

D = 768
HEADS = 12
HD = 64
FF = 3072
CAPTION = 128
REGIONS = 80
MB = 4
SEQ_MB = 4
SEQLEN = 208
SEQ_ALL = 16
LAYERS = 2
N_DP = 4


def touch_ends(values, rng, least, top_value):
    longest = values.shape.index(max(values.shape))
    spots = []
    for shift in (0, 1):
        where = [jax.random.randint(jax.random.fold_in(rng, axis), (), 0, length) for axis, length in enumerate(values.shape)]
        where[longest] = (where[longest] + shift) % values.shape[longest]
        spots.append(tuple(where))
    return values.at[spots[0]].set(least).at[spots[1]].set(top_value)


def level_of(key, extent, split, least, top_value):
    gain, own = 1.0, jax.random.fold_in(key, 6)
    for dim, parts in split:
        draws = jnp.exp(jax.random.uniform(jax.random.fold_in(own, dim), (parts,), jnp.float32, least / len(split), top_value / len(split)))
        gain = gain * jnp.repeat(draws, extent[dim] // parts).reshape([-1 if axis == dim else 1 for axis in range(len(extent))])
    return gain


def scatter_about(key, shape, deviation, most, split=(), kind=jnp.bfloat16):
    gain = level_of(key, shape, split, -0.22, 0.18) if split else 1.0
    result = jax.random.normal(key, shape, jnp.float32) * deviation * gain
    return jnp.minimum(jnp.maximum(result, -most), most).astype(kind)


def setup_inputs(seed: int = 0) -> dict:
    key_list = jax.random.split(jax.random.key(seed), 17)
    return {
        "layer_input": scatter_about(key_list[0], (MB, SEQ_ALL * SEQLEN, D), 1.0, 6.0, ((1, 16),)),
        "cotangent": scatter_about(key_list[1], (MB, SEQ_ALL * SEQLEN, D), 1.0, 6.0, ((1, 16),)),
        "region_count": touch_ends(jax.random.randint(key_list[2], (MB, SEQ_ALL), REGIONS // 8, REGIONS + 1), jax.random.fold_in(key_list[2], 1), REGIONS // 8, REGIONS).astype(jnp.int32),
        "region_mask": touch_ends((jax.random.randint(key_list[3], (MB, SEQ_ALL, REGIONS), 0, 4) < 3).astype(jnp.int32), jax.random.fold_in(key_list[3], 1), 0, 1),
        "attn_weight": scatter_about(key_list[4], (LAYERS, D, HEADS, 3 * HD), D ** -0.5, 0.21875, ((0, 2), (2, 4))),
        "attn_bias": scatter_about(key_list[5], (LAYERS, HEADS, 2 * HD), 0.1, 0.6, ((0, 2), (1, 4)), jnp.float32),
        "proj_weight": scatter_about(key_list[6], (LAYERS, HEADS, HD, D), (D // 48) ** -0.5, 1.5, ((0, 2), (1, 4))),
        "proj_bias": scatter_about(key_list[7], (LAYERS, D), 0.3, 1.8, ((0, 2),), jnp.float32),
        "first_gain": jnp.clip(1.0 + 0.1 * jax.random.normal(key_list[8], (LAYERS, D), jnp.float32), 0.5, 1.5),
        "first_shift": scatter_about(key_list[9], (LAYERS, D), 0.3, 1.8, ((0, 2),), jnp.float32),
        "up_weight": scatter_about(key_list[10], (LAYERS, D, FF), D ** -0.5, 0.21875, ((0, 2), (2, 4))),
        "up_bias": scatter_about(key_list[11], (LAYERS, FF), 0.3, 1.8, ((0, 2), (1, 4)), jnp.float32),
        "down_weight": scatter_about(key_list[12], (LAYERS, FF, D), FF ** -0.5, 0.109375, ((0, 2), (1, 4))),
        "down_bias": scatter_about(key_list[13], (LAYERS, D), 0.3, 1.8, ((0, 2),), jnp.float32),
        "second_gain": jnp.clip(1.0 + 0.1 * jax.random.normal(key_list[14], (LAYERS, D), jnp.float32), 0.5, 1.5),
        "second_shift": scatter_about(key_list[15], (LAYERS, D), 0.3, 1.8, ((0, 2),), jnp.float32),
    }


@jax.custom_vjp
def low(v):
    return lax.optimization_barrier(v.astype(jnp.bfloat16)).astype(jnp.float32)

@jax.custom_vjp
def low_back(v):
    return v

def low_keep(v):
    return (low(v), None)

def low_pass(kept, grad):
    return (grad,)

def back_keep(v):
    return (v, None)

def back_low(kept, grad):
    return (low(grad),)
low.defvjp(low_keep, low_pass)
low_back.defvjp(back_keep, back_low)
norm_eps = 1e-06
masked_value = -1000000000.0

def product(left, right):
    return jnp.dot(left, right, precision=lax.Precision.HIGHEST)

def layer_norm(residual, gain_vec, shift_vec):
    center = residual - lax.optimization_barrier(jnp.mean(residual, axis=-1, keepdims=True))
    spread = lax.optimization_barrier(jnp.mean(center * center, axis=-1, keepdims=True))
    return center * lax.rsqrt(spread + norm_eps) * gain_vec + shift_vec

def key_allowed(region_count, region_mask):
    regions = region_mask.shape[-1]
    slot_index = jnp.arange(CAPTION + regions, dtype=jnp.int32) - CAPTION
    caption_ones = jnp.ones(region_mask.shape[:-1] + (CAPTION,), jnp.int32)
    present = jnp.concatenate([caption_ones, region_mask], axis=-1) > 0
    return present & (slot_index < region_count[..., None])

def one_layer(group_rows, allowed, chosen):
    attn_w, attn_b, proj_w, proj_b, gain_one, shift_one, up_w, up_b, down_w, down_b, gain_two, shift_two = chosen
    sequences = group_rows.shape[0]
    flat = group_rows.reshape(-1, D)
    full_bias = jnp.concatenate([attn_b[:, :HD], jnp.zeros((HEADS, HD), jnp.float32), attn_b[:, HD:]], axis=1)
    projected = product(flat, attn_w.reshape(D, -1)).reshape(-1, HEADS, 3 * HD)
    projected = low_back(low(projected + full_bias))
    projected = projected.reshape(sequences, SEQLEN, HEADS, 3 * HD)
    queries = projected[..., :HD]
    key_rows = projected[..., HD:2 * HD]
    value_rows = projected[..., 2 * HD:]
    scores = jnp.einsum('sqhd,skhd->shqk', queries, key_rows, precision=lax.Precision.HIGHEST) * 0.125
    scores = low_back(scores)
    scores = jnp.where(allowed[:, None, None, :], scores, masked_value)
    weights_low = low(jax.nn.softmax(scores, axis=-1))
    context = jnp.einsum('shqk,skhd->sqhd', weights_low, value_rows, precision=lax.Precision.HIGHEST)
    context = low_back(low(context)).reshape(-1, HEADS * HD)
    attended = low_back(product(context, proj_w.reshape(HEADS * HD, D))) + proj_b
    hidden = layer_norm(flat + attended, gain_one, shift_one)
    hidden_low = low(hidden)
    upward = low_back(product(hidden_low, up_w) + up_b)
    activated = low(jax.nn.gelu(upward, approximate=False))
    feed = low_back(product(activated, down_w)) + down_b
    return layer_norm(hidden + feed, gain_two, shift_two).reshape(group_rows.shape)

def reference(layer_input, cotangent, region_count, region_mask, attn_weight, attn_bias, proj_weight, proj_bias, first_gain, first_shift, up_weight, up_bias, down_weight, down_bias, second_gain, second_shift):
    groups = MB * N_DP
    allowed = key_allowed(region_count, region_mask).reshape(groups, SEQ_MB, SEQLEN)
    start = layer_input.astype(jnp.float32).reshape(groups, SEQ_MB, SEQLEN, D)
    weights = tuple((member.astype(jnp.float32) for member in (attn_weight, attn_bias, proj_weight, proj_bias, first_gain, first_shift, up_weight, up_bias, down_weight, down_bias, second_gain, second_shift)))
    extra_zero = jnp.zeros_like(start)

    def forward(first_in, extra_in, *params):

        def run_layer(group_data, layer_no):
            chosen = [member[layer_no] for member in params]

            def group_fn(group_pair):
                return one_layer(group_pair[0], group_pair[1], chosen)
            return lax.map(jax.checkpoint(group_fn), (group_data, allowed))
        first_out = low(run_layer(first_in, 0))
        second_out = low(run_layer(low_back(first_out) + extra_in, 1))
        return (second_out, first_out)
    second_out, pullback, first_out = jax.vjp(forward, start, extra_zero, *weights, has_aux=True)
    grads = pullback(cotangent.astype(jnp.float32).reshape(start.shape))
    out_shape = (2, MB, SEQ_ALL * SEQLEN, D)
    layer_outputs = jnp.stack([first_out, second_out]).reshape(out_shape).astype(jnp.bfloat16)
    input_grads = jnp.stack([grads[0], grads[1]]).reshape(out_shape)
    return (layer_outputs, input_grads, grads[2], grads[3], grads[4], grads[5], grads[6], grads[7], grads[8], grads[9], grads[10], grads[11], grads[12], grads[13])
```

```python
import jax
import jax.numpy as jnp
from jax import lax
from jax.sharding import PartitionSpec as P

HD = 64
CAPTION = 128
SEQLEN = 208

norm_eps = 1e-06
masked_value = -1000000000.0
BF = jnp.bfloat16
F32 = jnp.float32


def layer_norm(residual, gain_vec, shift_vec):
    center = residual - jnp.mean(residual, axis=-1, keepdims=True)
    spread = jnp.mean(center * center, axis=-1, keepdims=True)
    return center * lax.rsqrt(spread + norm_eps) * gain_vec + shift_vec


def norm_parts(residual):
    center = residual - jnp.mean(residual, axis=-1, keepdims=True)
    rstd = lax.rsqrt(jnp.mean(center * center, axis=-1, keepdims=True) + norm_eps)
    return center * rstd, rstd


def norm_back(grad, normed, rstd, gain):
    g = grad * gain
    return rstd * (
        g
        - jnp.mean(g, axis=-1, keepdims=True)
        - normed * jnp.mean(g * normed, axis=-1, keepdims=True)
    )


def exact_gelu(inputs):
    return jax.nn.gelu(inputs, approximate=False)


def key_allowed(region_count, region_mask):
    regions = region_mask.shape[-1]
    slot_index = jnp.arange(CAPTION + regions, dtype=jnp.int32) - CAPTION
    caption_ones = jnp.ones(region_mask.shape[:-1] + (CAPTION,), jnp.int32)
    present = jnp.concatenate([caption_ones, region_mask], axis=-1) > 0
    return present & (slot_index < region_count[..., None])


def mm(a, b):
    return jnp.dot(a, b, preferred_element_type=F32)


def mm_t(a, b):
    return jnp.einsum("nf,df->nd", a, b, preferred_element_type=F32)


def mm_rows(a, b):
    return jnp.einsum("nf,nd->fd", a, b, preferred_element_type=F32)


def split_heads(projected, sequences):
    pieces = projected.reshape(sequences, SEQLEN, -1, 3, HD)
    return (pieces[:, :, :, 0], pieces[:, :, :, 1], pieces[:, :, :, 2])


def masked_scores(queries, key_rows, allowed):
    scores = jnp.einsum("sqhd,skhd->shqk", queries, key_rows, preferred_element_type=F32) * 0.125
    return jnp.where(allowed[:, None, None, :], scores, masked_value)


def forward_layer(rows_in, allowed, params):
    attn_w, full_bias, proj_w, proj_b, gain_one, shift_one, up_w, up_b, down_w, down_b, gain_two, shift_two = params
    sequences = allowed.shape[0]
    projected = (mm(rows_in, attn_w) + full_bias).astype(BF)
    queries, key_rows, value_rows = split_heads(projected, sequences)
    scores = masked_scores(queries, key_rows, allowed)
    row_max = jnp.max(scores, axis=-1, keepdims=True)
    exp_scores = jnp.exp(scores - row_max)
    row_sum = jnp.sum(exp_scores, axis=-1, keepdims=True)
    weights_bf = (exp_scores / row_sum).astype(BF)
    log_total = row_max + jnp.log(row_sum)
    context = jnp.einsum("shqk,skhd->sqhd", weights_bf, value_rows, preferred_element_type=F32)
    context = context.astype(BF).reshape(rows_in.shape[0], -1)
    resid_one = rows_in.astype(F32) + mm(context, proj_w) + proj_b
    hidden = layer_norm(resid_one, gain_one, shift_one)
    middle = hidden.astype(BF)
    upward = mm(middle, up_w) + up_b
    activated = exact_gelu(upward).astype(BF)
    resid_two = hidden + mm(activated, down_w) + down_b
    output = layer_norm(resid_two, gain_two, shift_two).astype(BF)
    saved = (rows_in, projected, log_total, context, resid_one, middle, upward, activated, resid_two, allowed)
    return output, saved


def backward_layer(grad_out, saved, params, full):
    attn_w, full_bias, proj_w, proj_b, gain_one, shift_one, up_w, up_b, down_w, down_b, gain_two, shift_two = params
    rows_in, projected, log_total, context, resid_one, middle, upward, activated, resid_two, allowed = saved
    sequences = allowed.shape[0]
    n_two, r_two = norm_parts(resid_two)
    d_resid_two = norm_back(grad_out, n_two, r_two, gain_two)
    feed_rows = d_resid_two.astype(BF)
    d_activated = mm_t(feed_rows, down_w)
    _, gelu_back = jax.vjp(exact_gelu, upward)
    d_upward = gelu_back(d_activated)[0].astype(BF)
    d_hidden = d_resid_two + mm_t(d_upward, up_w)
    n_one, r_one = norm_parts(resid_one)
    d_resid_one = norm_back(d_hidden, n_one, r_one, gain_one)
    attn_rows = d_resid_one.astype(BF)
    d_context = mm_t(attn_rows, proj_w).astype(BF)
    queries, key_rows, value_rows = split_heads(projected, sequences)
    d_context = d_context.reshape(queries.shape)
    scores = masked_scores(queries, key_rows, allowed)
    probs_full = jnp.exp(scores - log_total)
    weights_bf = probs_full.astype(BF)
    d_values = jnp.einsum("shqk,sqhd->skhd", weights_bf, d_context, preferred_element_type=F32)
    d_weights = jnp.einsum("sqhd,skhd->shqk", d_context, value_rows, preferred_element_type=F32)
    d_scores = probs_full * (d_weights - jnp.sum(d_weights * probs_full, axis=-1, keepdims=True))
    d_scores = d_scores.astype(BF)
    d_queries = jnp.einsum("shqk,skhd->sqhd", d_scores, key_rows, preferred_element_type=F32) * 0.125
    d_keys = jnp.einsum("shqk,sqhd->skhd", d_scores, queries, preferred_element_type=F32) * 0.125
    d_projected = jnp.stack([d_queries, d_keys, d_values], axis=3).reshape(projected.shape).astype(BF)
    d_rows = d_resid_one + mm_t(d_projected, attn_w)
    if not full:
        return d_rows, None
    grads = dict(
        down=mm_rows(activated, feed_rows).astype(BF),
        up=mm_rows(middle, d_upward).astype(BF),
        proj=mm_rows(context, attn_rows).astype(BF),
        attn=mm_rows(rows_in, d_projected).astype(BF),
        attn_bias=jnp.sum(d_projected.astype(F32), axis=0),
        up_bias=jnp.sum(d_upward.astype(F32), axis=0),
        gain_two=jnp.sum(grad_out * n_two, axis=0),
        shift_two=jnp.sum(grad_out, axis=0),
        down_bias=jnp.sum(d_resid_two, axis=0),
        gain_one=jnp.sum(d_hidden * n_one, axis=0),
        shift_one=jnp.sum(d_hidden, axis=0),
        proj_bias=jnp.sum(d_resid_one, axis=0),
    )
    return d_rows, grads


def swapped(value, axis, bit):
    count = lax.axis_size(axis)
    return lax.ppermute(value, axis, [(i, i ^ bit) for i in range(count)])


def chain_sum(value, axis):
    count = lax.axis_size(axis)
    if count == 1:
        return value
    if count % 2:
        return lax.psum(value, axis)
    here = lax.axis_index(axis)
    half = count // 2
    for step in range(half - 1):
        got = lax.ppermute(value, axis, [(step, step + 1), (count - 1 - step, count - 2 - step)])
        takes = (here == step + 1) | (here == count - 2 - step)
        value = jnp.where(takes, value + got, value)
    got = lax.ppermute(value, axis, [(half - 1, half), (half, half - 1)])
    value = value + got
    for step in range(half - 1, 0, -1):
        got = lax.ppermute(value, axis, [(step, step - 1), (count - 1 - step, count - step)])
        takes = (here == step - 1) | (here == count - step)
        value = jnp.where(takes, got, value)
    return value


def gathered(value):
    far = swapped(value, "tensor", 2)
    return [value, swapped(value, "tensor", 1), far, swapped(far, "tensor", 1)]


def scattered(parts):
    own, near, far, both = parts
    keep = own + swapped(near, "tensor", 1)
    send = far + swapped(both, "tensor", 1)
    return keep + swapped(send, "tensor", 2)


def body(
    layer_input, cotangent, region_count, region_mask, attn_weight, attn_bias, proj_weight, proj_bias,
    first_gain, first_shift, up_weight, up_bias, down_weight, down_bias, second_gain, second_shift,
):
    section = lax.axis_index("section")
    tensor = lax.axis_index("tensor")
    micro, rows, width = layer_input.shape
    local_heads = attn_weight.shape[2]
    local_units = up_weight.shape[2]
    ranks = lax.axis_size("tensor")
    assert rows == SEQLEN and ranks == 4

    pieces = attn_bias[0].reshape(local_heads, 2, -1)
    own_bias = jnp.stack([pieces[:, 0], jnp.zeros_like(pieces[:, 0]), pieces[:, 1]], axis=1).reshape(-1)
    small = jnp.concatenate([own_bias, up_bias[0]]).reshape(1, -1)
    smalls = gathered(small)
    cut = own_bias.shape[0]
    full_bias = jnp.concatenate([s[0, :cut] for s in smalls])
    unit_bias = jnp.concatenate([s[0, cut:] for s in smalls])
    attn_w = jnp.concatenate(gathered(attn_weight[0].reshape(width, -1)), axis=1)
    proj_w = jnp.concatenate(gathered(proj_weight[0].reshape(-1, width)), axis=0)
    up_w = jnp.concatenate(gathered(up_weight[0]), axis=1)
    down_w = jnp.concatenate(gathered(down_weight[0]), axis=0)
    params = (
        attn_w, full_bias, proj_w, proj_bias[0], first_gain[0], first_shift[0],
        up_w, unit_bias, down_w, down_bias[0], second_gain[0], second_shift[0],
    )
    allowed = lax.dynamic_index_in_dim(key_allowed(region_count, region_mask), tensor, 1, False)

    own_rows = layer_input.reshape(micro * rows, width)
    out_one, _ = forward_layer(own_rows, allowed, params)
    received = lax.ppermute(out_one, "section", [(0, 1)])
    rows_in = jnp.where(section == 0, own_rows, received)
    output, saved = forward_layer(rows_in, allowed, params)
    saved = lax.optimization_barrier(saved)
    cot = cotangent.reshape(micro * rows, width)
    d_first, _ = backward_layer(cot.astype(F32), saved, params, False)
    sent = lax.ppermute(d_first.astype(BF), "section", [(1, 0)])
    grad_in = jnp.where(section == 1, cot, sent).astype(F32)
    d_rows, grads = backward_layer(grad_in, saved, params, True)

    def column_parts(value):
        size = value.shape[1] // ranks
        return [value[:, r * size:(r + 1) * size] for r in range(ranks)]

    def row_parts(value):
        size = value.shape[0] // ranks
        return [value[r * size:(r + 1) * size] for r in range(ranks)]

    def total(parts):
        return chain_sum(scattered(parts), "dp").astype(F32)

    g_down = total(row_parts(grads["down"]))
    g_up = total(column_parts(grads["up"]))
    g_proj = total(row_parts(grads["proj"]))
    g_attn = total(column_parts(grads["attn"]))

    def canonical(vector):
        quarters = vector.reshape(ranks, -1)
        return jnp.concatenate([lax.dynamic_index_in_dim(quarters, q ^ tensor, 0, False) for q in range(ranks)])

    names = ("proj_bias", "gain_one", "shift_one", "down_bias", "gain_two", "shift_two")
    flat = jnp.concatenate([grads[k] for k in names] + [canonical(grads["attn_bias"]), canonical(grads["up_bias"])])
    flat = lax.psum(flat, ("dp", "tensor"))
    rowed = {k: flat[i * width:(i + 1) * width] for i, k in enumerate(names)}
    base = len(names) * width
    bias_sum = lax.dynamic_slice_in_dim(flat, base + tensor * cut, cut).reshape(local_heads, 3, -1)
    grad_attn_bias = jnp.concatenate([bias_sum[:, 0], bias_sum[:, 2]], axis=1)
    g_up_bias = lax.dynamic_slice_in_dim(flat, base + ranks * cut + tensor * local_units, local_units)
    return (
        output.reshape(1, micro, rows, width),
        d_rows.reshape(1, micro, rows, width),
        g_attn.reshape(attn_weight.shape),
        grad_attn_bias[None],
        g_proj.reshape(proj_weight.shape),
        rowed["proj_bias"][None],
        rowed["gain_one"][None],
        rowed["shift_one"][None],
        g_up[None],
        g_up_bias[None],
        g_down[None],
        rowed["down_bias"][None],
        rowed["gain_two"][None],
        rowed["shift_two"][None],
    )


def solution(mesh):
    placed = (
        P(None, ("dp", "tensor"), None),
        P(None, ("dp", "tensor"), None),
        P(None, "dp"),
        P(None, "dp", None),
        P("section", None, "tensor", None),
        P("section", "tensor", None),
        P("section", "tensor", None, None),
        P("section", None),
        P("section", None),
        P("section", None),
        P("section", None, "tensor"),
        P("section", "tensor"),
        P("section", "tensor", None),
        P("section", None),
        P("section", None),
        P("section", None),
    )
    return jax.shard_map(
        body,
        mesh=mesh,
        in_specs=placed,
        out_specs=(
            P("section", None, ("dp", "tensor"), None),
            P("section", None, ("dp", "tensor"), None),
            P("section", None, "tensor", None),
            P("section", "tensor", None),
            P("section", "tensor", None, None),
            P("section", None),
            P("section", None),
            P("section", None),
            P("section", None, "tensor"),
            P("section", "tensor"),
            P("section", "tensor", None),
            P("section", None),
            P("section", None),
            P("section", None),
        ),
        check_vma=False,
    )
```

```python
import functools

import jax
import jax.numpy as jnp
from jax import lax
from jax.experimental import pallas as pl
from jax.experimental.pallas import tpu as pltpu
from jax.sharding import PartitionSpec as P

HD = 64
SEQLEN = 208
norm_eps = 1e-06
masked_value = -1000000000.0
BF = jnp.bfloat16
F32 = jnp.float32
NT = (((1,), (1,)), ((), ()))
TN = (((0,), (0,)), ((), ()))
MIB = 1 << 20
PARTS = 3
EXTRA = 32


def dot(a, b):
    return jnp.dot(a, b, preferred_element_type=F32)


def dot_nt(a, b):
    return lax.dot_general(a, b, NT, preferred_element_type=F32)


def dot_tn(a, b):
    return lax.dot_general(a, b, TN, preferred_element_type=F32)


def normed(residual):
    center = residual - jnp.mean(residual, axis=-1, keepdims=True)
    rstd = lax.rsqrt(jnp.mean(center * center, axis=-1, keepdims=True) + norm_eps)
    return center * rstd, rstd


def norm_back(grad, n, rstd, gain):
    g = grad * gain
    return rstd * (g - jnp.mean(g, axis=-1, keepdims=True) - n * jnp.mean(g * n, axis=-1, keepdims=True))


def gelu_parts(u, slope):
    size = jnp.abs(u)
    t = pl.reciprocal(1.0 + 0.23164189 * size, approx=True)
    poly = t * (0.127414796 + t * (-0.142248368 + t * (0.7107068705 + t * (-0.7265760135 + t * 0.5307027145))))
    bell = jnp.exp2(u * (u * -0.7213475204444817))
    tail = poly * bell
    act = jnp.maximum(u, 0.0) - size * tail
    if not slope:
        return act, None
    return act, jnp.where(u < 0, tail, 1.0 - tail) + u * (bell * 0.3989422804014327)


def fixed(a):
    return pl.BlockSpec(a.shape, lambda q: (0,) * len(a.shape))


def quarter(a):
    return pl.BlockSpec((1,) + tuple(a.shape[1:]), lambda q: (q,) + (0,) * (len(a.shape) - 1))


def call(kernel, name, count, ins, outs, scratch, flops, limit=24):
    spec = lambda pair: (quarter if pair[1] else fixed)(pair[0])
    size = sum(a.size * a.dtype.itemsize for a, _ in (*ins, *outs))
    return pl.pallas_call(
        kernel,
        grid=(count,),
        in_specs=[spec(p) for p in ins],
        out_specs=[spec(p) for p in outs],
        out_shape=[a for a, _ in outs],
        scratch_shapes=scratch,
        compiler_params=pltpu.CompilerParams(vmem_limit_bytes=limit * MIB),
        cost_estimate=pl.CostEstimate(flops=2 * flops, bytes_accessed=size, transcendentals=0),
        name=name,
    )(*[a for a, _ in ins])


def shape(*dims, t=BF):
    return jax.ShapeDtypeStruct(dims, t)


def units_of(p, seqs):
    for s in range(seqs):
        for h in range(p.shape[1] // (3 * HD)):
            yield s, h


def head_rows(p, s, h, part):
    at = (3 * h + part) * HD
    return p[s * SEQLEN:(s + 1) * SEQLEN, at:at + HD]


def attn_fwd_kernel(save, first, seqs, x_ref, ok_ref, base_ref, ab_ref, wt_ref, pw_ref, r1_ref, *saved):
    q = pl.program_id(0)
    x = x_ref[...]

    @pl.when(q == 0)
    def _():
        r1_ref[...] = x.astype(F32) + base_ref[...] if first else base_ref[...]

    cols = ab_ref.shape[2]
    p = (dot_nt(x, wt_ref[0, :cols]) + ab_ref[0]).astype(BF)
    blocks = list(units_of(p, seqs))
    oks = [ok_ref[s] > 0 for s in range(seqs)]
    scores = [dot_nt(head_rows(p, s, h, 1), head_rows(p, s, h, 0) * 0.125) for s, h in blocks]
    probs = []
    for (s, h), st in zip(blocks, scores):
        st = jnp.where(oks[s], st, masked_value)
        e = jnp.exp(st - jnp.max(st, axis=0, keepdims=True))
        probs.append((e * (1.0 / jnp.sum(e, axis=0, keepdims=True))).astype(BF))
    cts = [dot_tn(head_rows(p, s, h, 2), a).astype(BF) for (s, h), a in zip(blocks, probs)]
    per = len(blocks) // seqs
    c = jnp.concatenate([jnp.concatenate(cts[s * per:(s + 1) * per], axis=0).T for s in range(seqs)], axis=0)
    r1_ref[...] += dot(c, pw_ref[0])
    if save:
        saved[0][0] = p
        saved[1][0] = c
        for (s, h), a in zip(blocks, probs):
            saved[2][0, s, h] = a


def attn_fwd(x, ok, base, ab, wt, pw, save, first):
    rows, width = x.shape
    count, _, cols = ab.shape
    seqs, heads = rows // SEQLEN, cols // (3 * HD)
    outs = [(shape(rows, width, t=F32), False)]
    if save:
        outs += [(shape(count, rows, cols), True), (shape(count, rows, heads * HD), True),
                 (shape(count, seqs, heads, SEQLEN, SEQLEN), True)]
    flops = count * 2 * rows * (width * cols + heads * HD * (2 * SEQLEN + width))
    ins = [(x, False), (ok, False), (base, False), (ab, True), (wt, True), (pw, True)]
    return call(functools.partial(attn_fwd_kernel, save, first, seqs), "attn_fwd", count, ins, outs, [], flops)


def ffn_fwd_kernel(save, first, last, x_ref, acc_in, vec_ref, ub_ref, up_ref, down_ref, *outs):
    q = pl.program_id(0)
    outs, (hb_ref, acc_ref) = outs[:-2], outs[-2:]

    @pl.when(q == 0)
    def _():
        if first:
            h = normed(x_ref[...])[0] * vec_ref[0:1] + vec_ref[1:2]
            hb_ref[...] = h.astype(BF)
            acc_ref[...] = h + vec_ref[2:3]
        else:
            hb_ref[...] = x_ref[...]
            acc_ref[...] = acc_in[...]

    hb = hb_ref[...]
    units = up_ref.shape[2]
    step = units // PARTS
    us = [dot(hb, up_ref[0, :, j * step:(j + 1) * step]) for j in range(PARTS)]
    es, slopes = [], []
    for j, u in enumerate(us):
        act, slope = gelu_parts(u + ub_ref[0, :, j * step:(j + 1) * step], save)
        es.append(act.astype(BF))
        if save:
            outs[2][0, :, j * step:(j + 1) * step] = slope.astype(BF)
    e = jnp.concatenate(es, axis=1)
    if save:
        outs[1][0] = e
    acc_ref[...] += dot(e, down_ref[0])

    @pl.when(q == pl.num_programs(0) - 1)
    def _():
        acc = acc_ref[...]
        if last:
            outs[0][...] = (normed(acc)[0] * vec_ref[3:4] + vec_ref[4:5]).astype(BF)
            if save:
                outs[3][...] = acc
                outs[4][...] = hb
        else:
            outs[0][...] = acc
            outs[1][...] = hb


def ffn_fwd(x, acc, vec, ub, up, down, save, first, last):
    rows, width = x.shape
    count, _, units = ub.shape
    outs = [(shape(rows, width, t=BF if last else F32), False)]
    if save:
        outs += [(shape(count, rows, units), True)] * 2 + [(shape(rows, width, t=F32), False), (shape(rows, width), False)]
    if not last:
        outs += [(shape(rows, width), False)]
    ins = [(x, False), (acc, False), (vec, False), (ub, True), (up, True), (down, True)]
    scratch = [pltpu.VMEM((rows, width), BF), pltpu.VMEM((rows, width), F32)]
    return call(functools.partial(ffn_fwd_kernel, save, first, last), "ffn_fwd", count, ins, outs, scratch,
                count * 4 * rows * width * units)


def ffn_bwd_kernel(full, dy_ref, r2_ref, r1_ref, vec_ref, slope_ref, up_ref, down_ref, *outs):
    q = pl.program_id(0)
    outs, (df_ref, dh_ref, sum_ref) = outs[:-3], outs[-3:]
    total = lambda v: jnp.sum(v, axis=0, keepdims=True)

    @pl.when(q == 0)
    def _():
        dy = dy_ref[...].astype(F32)
        n2, s2 = normed(r2_ref[...])
        dr2 = norm_back(dy, n2, s2, vec_ref[3:4])
        df_ref[...] = dr2.astype(BF)
        dh_ref[...] = dr2
        if full:
            sum_ref[0:1] = total(dr2)
            sum_ref[1:2] = total(dy * n2)
            sum_ref[2:3] = total(dy)

    df = df_ref[...]
    units = up_ref.shape[2]
    step = units // PARTS
    des = [dot_nt(df, down_ref[0, j * step:(j + 1) * step]) for j in range(PARTS)]
    dus = [(de * slope_ref[0, :, j * step:(j + 1) * step].astype(F32)).astype(BF) for j, de in enumerate(des)]
    du = jnp.concatenate(dus, axis=1)
    dh_ref[...] += dot_nt(du, up_ref[0])
    if full:
        outs[3][0] = du
        outs[4][0] = total(du.astype(F32))

    @pl.when(q == pl.num_programs(0) - 1)
    def _():
        dh = dh_ref[...]
        n1, s1 = normed(r1_ref[...])
        dr1 = norm_back(dh, n1, s1, vec_ref[0:1])
        outs[0][...] = dr1
        outs[1][...] = dr1.astype(BF)
        if full:
            outs[2][...] = df
            outs[5][0:1] = total(dr1)
            outs[5][1:2] = total(dh * n1)
            outs[5][2:3] = total(dh)
            outs[5][3:6] = sum_ref[0:3]
            outs[5][6:8] = jnp.zeros_like(outs[5][6:8])


def ffn_bwd(dy, r2, r1, vec, slope, up, down, full):
    rows, width = r1.shape
    count, _, units = slope.shape
    outs = [(shape(rows, width, t=F32), False), (shape(rows, width), False)]
    if full:
        outs += [(shape(rows, width), False), (shape(count, rows, units), True),
                 (shape(count, 1, units, t=F32), True), (shape(8, width, t=F32), False)]
    ins = [(dy, False), (r2, False), (r1, False), (vec, False), (slope, True), (up, True), (down, True)]
    scratch = [pltpu.VMEM((rows, width), BF), pltpu.VMEM((rows, width), F32), pltpu.VMEM((8, width), F32)]
    return call(functools.partial(ffn_bwd_kernel, full), "ffn_bwd", count, ins, outs, scratch,
                count * 4 * rows * width * units)


def attn_bwd_kernel(full, seqs, dg_ref, dr1_ref, p_ref, a_ref, wt_ref, pw_ref, *outs):
    q = pl.program_id(0)
    outs, dx_ref = outs[:-1], outs[-1]

    @pl.when(q == 0)
    def _():
        dx_ref[...] = dr1_ref[...]

    dc = dot_nt(dg_ref[...], pw_ref[0]).astype(BF)
    p = p_ref[0]
    blocks = list(units_of(p, seqs))
    dcs = [dc[s * SEQLEN:(s + 1) * SEQLEN, h * HD:(h + 1) * HD] for s, h in blocks]
    das = [dot_nt(head_rows(p, s, h, 2), d) for (s, h), d in zip(blocks, dcs)]
    dss = []
    for (s, h), da in zip(blocks, das):
        a = a_ref[0, s, h].astype(F32)
        dss.append((a * (da - jnp.sum(da * a, axis=0, keepdims=True))).astype(BF))
    pieces = []
    for (s, h), d, ds in zip(blocks, dcs, dss):
        dq = dot_tn(ds, head_rows(p, s, h, 1)) * 0.125
        dk = dot(ds, head_rows(p, s, h, 0)) * 0.125
        dv = dot(a_ref[0, s, h], d)
        pieces += [dq.astype(BF), dk.astype(BF), dv.astype(BF)]
    per = len(pieces) // seqs
    dp = jnp.concatenate([jnp.concatenate(pieces[s * per:(s + 1) * per], axis=1) for s in range(seqs)], axis=0)
    dx_ref[...] += dot(dp, wt_ref[0, :dp.shape[1]])
    if full:
        outs[1][0] = dp
        outs[2][0] = jnp.sum(dp.astype(F32), axis=0, keepdims=True)

    @pl.when(q == pl.num_programs(0) - 1)
    def _():
        outs[0][...] = dx_ref[...].astype(outs[0].dtype)


def attn_bwd(dg, dr1, p, a, wt, pw, full):
    rows, width = dg.shape
    count, _, cols = p.shape
    seqs, heads = rows // SEQLEN, cols // (3 * HD)
    outs = [(shape(rows, width, t=F32 if full else BF), False)]
    if full:
        outs += [(shape(count, rows, cols), True), (shape(count, 1, cols, t=F32), True)]
    ins = [(dg, False), (dr1, False), (p, True), (a, True), (wt, True), (pw, True)]
    flops = count * 2 * rows * (width * cols + heads * HD * (4 * SEQLEN + width))
    return call(functools.partial(attn_bwd_kernel, full, seqs), "attn_bwd", count, ins, outs,
                [pltpu.VMEM((rows, width), F32)], flops)


def wgrad_kernel(pairs, added, *refs):
    total = None
    for g in range(pairs):
        a, b = refs[2 * g], refs[2 * g + 1]
        a = a[0] if len(a.shape) == 3 else a[...]
        b = b[0] if len(b.shape) == 3 else b[...]
        part = dot_tn(a, b)
        total = part if total is None else total + part
    if added:
        total = total + refs[2 * pairs][0].astype(F32)
    refs[-1][0] = total.astype(BF)


def wgrad(pairs, odd, more=None):
    def spec(a):
        if a.ndim == 2:
            return pl.BlockSpec(a.shape, lambda i: (0, 0))
        return pl.BlockSpec((1,) + a.shape[1:], lambda i: (2 * i + odd, 0, 0))

    flat = [a for pair in pairs for a in pair]
    dims = (2, pairs[0][0].shape[-1], pairs[0][1].shape[-1])
    block = pl.BlockSpec((1,) + dims[1:], lambda i: (i, 0, 0))
    extra = [] if more is None else [more]
    rows = sum(a.shape[-2] for a, _ in pairs)
    return pl.pallas_call(
        functools.partial(wgrad_kernel, len(pairs), more is not None),
        grid=(2,),
        in_specs=[spec(a) for a in flat] + [block] * len(extra),
        out_specs=block,
        out_shape=shape(*dims),
        compiler_params=pltpu.CompilerParams(vmem_limit_bytes=24 * MIB),
        cost_estimate=pl.CostEstimate(flops=8 * rows * dims[1] * dims[2], bytes_accessed=8 * MIB, transcendentals=0),
        name="wgrad",
    )(*flat, *extra)


def swapped(value, axis, bit):
    count = lax.axis_size(axis)
    return lax.ppermute(value, axis, [(i, i ^ bit) for i in range(count)])


def near(value):
    return swapped(value, "tensor", 1)


def over_y(value):
    return swapped(value, "tensor", 2)


def chain_steps(count):
    half = count // 2
    inward = [[(s, s + 1), (count - 1 - s, count - 2 - s)] for s in range(half - 1)]
    outward = [[(s, s - 1), (count - 1 - s, count - s)] for s in range(half - 1, 0, -1)]
    return inward, [(half - 1, half), (half, half - 1)], outward


def chain_sum(value, axis):
    count = lax.axis_size(axis)
    if count == 1:
        return value
    if count % 2:
        return lax.psum(value, axis)
    here = lax.axis_index(axis)
    inward, cross, outward = chain_steps(count)
    for step in inward:
        value = value + lax.ppermute(value, axis, step)
    value = value + lax.ppermute(value, axis, cross)
    for step in outward:
        got = lax.ppermute(value, axis, step)
        takes = (here == step[0][1]) | (here == step[1][1])
        value = jnp.where(takes, got, value)
    return value


def after(value, *others):
    return lax.optimization_barrier((value, *others))[0]


def key_allowed(region_count, region_mask, caption):
    regions = region_mask.shape[-1]
    slot_index = jnp.arange(caption + regions, dtype=jnp.int32) - caption
    caption_ones = jnp.ones(region_mask.shape[:-1] + (caption,), jnp.int32)
    present = jnp.concatenate([caption_ones, region_mask], axis=-1) > 0
    return present & (slot_index < region_count[..., None])


def three_parts(vector):
    high = lax.reduce_precision(vector, 8, 7)
    mid = lax.reduce_precision(vector - high, 8, 7)
    return [high, mid, vector - high - mid]


def body(
    layer_input, cotangent, region_count, region_mask, attn_weight, attn_bias, proj_weight, proj_bias,
    first_gain, first_shift, up_weight, up_bias, down_weight, down_bias, second_gain, second_shift,
):
    section = lax.axis_index("section")
    tensor = lax.axis_index("tensor")
    micro, rows, width = layer_input.shape
    heads = attn_weight.shape[2]
    cols = heads * attn_weight.shape[3]
    units = up_weight.shape[2]
    assert rows == SEQLEN and lax.axis_size("tensor") == 4
    dp_pairs = lax.axis_size("dp") % 2 == 0
    odd = lax.axis_index("dp") % 2 == 1

    pieces = attn_bias[0].reshape(heads, 2, -1)
    own_bias = jnp.stack([pieces[:, 0], jnp.zeros_like(pieces[:, 0]), pieces[:, 1]], axis=1).reshape(-1)
    own_bias = jnp.pad(own_bias, (0, width - cols))
    tail = jnp.stack(three_parts(own_bias) + three_parts(up_bias[0])).astype(BF)
    tail = after(jnp.pad(tail, ((0, EXTRA - 6), (0, 0))))
    attn_own = attn_weight[0].transpose(1, 2, 0).reshape(cols, width)
    attn_own = jnp.concatenate([attn_own, tail], axis=0)
    proj_own = proj_weight[0].reshape(-1, width)
    up_own = up_weight[0]
    down_own = down_weight[0]

    def part(own):
        half = own.shape[0] // 2
        return jnp.where(odd, own[half:], own[:half]) if dp_pairs else own

    def along_dp(mine):
        return swapped(mine, "dp", 1) if dp_pairs else mine

    def both_halves(mine, pair):
        if not dp_pairs:
            return mine
        return jnp.where(odd, jnp.concatenate([pair, mine]), jnp.concatenate([mine, pair]))

    def pair_of(a, b):
        return jnp.stack([a, b])

    ok = lax.dynamic_index_in_dim(key_allowed(region_count, region_mask, rows - region_mask.shape[-1]), tensor, 1, False)
    ok = ok.astype(jnp.int32)[:, :, None]
    vec = jnp.concatenate([first_gain, first_shift, down_bias, second_gain, second_shift], axis=0)
    groups = 2 if micro % 2 == 0 else 1
    per = micro // groups
    size = per * rows
    cut = lambda value: [value.reshape(micro * rows, -1)[g * size:(g + 1) * size] for g in range(groups)]
    oks = [ok[g * per:(g + 1) * per] for g in range(groups)]
    x_own, cots = cut(layer_input), cut(cotangent)

    attn_mine = over_y(part(attn_own))
    attn_near = near(attn_own)
    proj_mine = over_y(after(part(proj_own), attn_near))
    proj_near = near(proj_own)
    up_mine = over_y(after(part(up_own), attn_mine))
    attn_pair = along_dp(attn_mine)
    up_near = near(after(up_own, proj_near))
    down_mine = over_y(after(part(down_own), proj_mine))
    proj_pair = along_dp(proj_mine)
    down_near = near(after(down_own, up_near))
    up_pair = along_dp(up_mine)
    down_pair = along_dp(down_mine)

    def biases(stack):
        three = stack[:, cols:cols + 6].astype(F32)
        return jnp.sum(three[:, :3], axis=1, keepdims=True)[:, :, :cols], jnp.sum(three[:, 3:], axis=1, keepdims=True)

    attn_0 = pair_of(attn_own, attn_near)
    proj_0 = pair_of(proj_own, proj_near)
    up_0 = pair_of(up_own, up_near)
    down_0 = pair_of(down_own, down_near)
    ab_0, ub_0 = biases(attn_0)
    r1s = [attn_fwd(x_own[g], oks[g], proj_bias, ab_0, attn_0, proj_0, False, True)[0] for g in range(groups)]
    attn_far = both_halves(attn_mine, attn_pair)
    attn_1 = pair_of(attn_far, near(attn_far))
    proj_far = both_halves(proj_mine, proj_pair)
    proj_1 = pair_of(proj_far, near(proj_far))
    ab_1, ub_1 = biases(attn_1)
    r1s = [attn_fwd(x_own[g], oks[g], r1s[g], ab_1, attn_1, proj_1, False, False)[0] for g in range(groups)]
    halves = [ffn_fwd(r1s[g], vec, vec, ub_0, up_0, down_0, False, True, False) for g in range(groups)]
    up_far = both_halves(up_mine, up_pair)
    up_1 = pair_of(up_far, near(up_far))
    down_far = both_halves(down_mine, down_pair)
    down_1 = pair_of(down_far, near(down_far))
    firsts, hops = [], []
    for g in range(groups):
        tok = firsts[-1:]
        acc, hb = halves[g]
        firsts.append(ffn_fwd(hb, after(acc, *tok), vec, ub_1, up_1, down_1, False, False, True)[0])
        hops.append(lax.ppermute(firsts[g], "section", [(0, 1)]))

    tok = firsts[-1]
    attn_w = jnp.concatenate([after(attn_0, tok), attn_1])
    proj_w = jnp.concatenate([after(proj_0, tok), proj_1])
    up_w = jnp.concatenate([after(up_0, tok), up_1])
    down_w = jnp.concatenate([after(down_0, tok), down_1])
    ab = jnp.concatenate([ab_0, ab_1])
    ub = jnp.concatenate([ub_0, ub_1])

    kept, outputs, backs = [], [], []
    tok = (up_w, down_w)
    for g in range(groups):
        x = jnp.where(section == 0, after(x_own[g], *tok), hops[g])
        r1, p, c, a = attn_fwd(x, oks[g], proj_bias, ab, attn_w, proj_w, True, True)
        y, e, slope, r2, hb = ffn_fwd(r1, vec, vec, ub, up_w, down_w, True, True, True)
        dr1, dg = ffn_bwd(cots[g], r2, r1, vec, slope, up_w, down_w, False)
        (d_first,) = attn_bwd(dg, dr1, p, a, attn_w, proj_w, False)
        backs.append(lax.ppermute(d_first, "section", [(1, 0)]))
        kept.append((x, r1, p, c, a, e, slope, r2, hb))
        outputs.append(y)
        tok = (d_first,)

    def ffn_part(g, *before):
        x, r1, p, c, a, e, slope, r2, hb = kept[g]
        dy = jnp.where(section == 1, after(cots[g], *before), backs[g])
        return ffn_bwd(dy, r2, r1, vec, slope, up_w, down_w, True)

    def attn_part(g, dg, dr1):
        x, r1, p, c, a, e, slope, r2, hb = kept[g]
        return attn_bwd(dg, dr1, p, a, attn_w, proj_w, True)

    ffn_parts, attn_parts = [], []
    for g in range(groups):
        ffn_parts.append(ffn_part(g, *tok))
        if g < groups - 1:
            attn_parts.append(attn_part(g, ffn_parts[g][1], ffn_parts[g][0]))
            tok = (attn_parts[g][0],)
    all_of = lambda a, b: [(a(g), b(g)) for g in range(groups)]
    down_terms = all_of(lambda g: kept[g][5], lambda g: ffn_parts[g][2])
    up_terms = all_of(lambda g: kept[g][8], lambda g: ffn_parts[g][3])
    proj_terms = all_of(lambda g: kept[g][3], lambda g: ffn_parts[g][1])

    def following(terms, *before):
        return [(after(terms[0][0], *before), terms[0][1])] + terms[1:]

    out_d = wgrad(down_terms, 1)
    got_d = near(out_d)
    out_u = wgrad(following(up_terms, out_d), 1)
    got_u = near(out_u)
    held_d = wgrad(following(down_terms, out_u), 0, got_d)
    held_u = wgrad(following(up_terms, held_d), 0, got_u)
    out_p = wgrad(following(proj_terms, held_u), 1)
    got_p = near(out_p)
    g = groups - 1
    attn_parts.append(attn_part(g, after(ffn_parts[g][1], out_p), ffn_parts[g][0]))
    attn_terms = all_of(lambda g: attn_parts[g][1], lambda g: kept[g][0])
    out_a = wgrad(attn_terms, 1)
    got_a = near(out_a)
    held_p = wgrad(following(proj_terms, out_a), 0, got_p)
    held_a = wgrad(following(attn_terms, held_p), 0, got_a)
    half, half_u, half_a = units // 2, width // 2, cols // 2
    owned = [(held_d, 0, half), (held_d, half, units), (held_u, 0, half_u), (held_u, half_u, width),
             (held_a, 0, half_a), (held_a, half_a, cols), (held_p, 0, held_p.shape[1])]
    count = len(owned)
    sent, mine = {}, {}
    for k, (held, lo, hi) in enumerate(owned):
        ahead = [mine[k - 2]] if k >= 2 else [sent[k - 1]] if False else []
        sent[k] = over_y(after(held[1, lo:hi], *ahead))
        base = after(held, attn_parts[-1][0], *([mine[k - 1]] if k else []))
        mine[k] = base[0, lo:hi] + sent[k]

    bias_sums = sum(part[2] for part in attn_parts)
    unit_sums = sum(part[4] for part in ffn_parts)
    row_sums = sum(part[5] for part in ffn_parts)[:6].reshape(1, 1, -1)
    small = jnp.concatenate([bias_sums, unit_sums, jnp.broadcast_to(row_sums, (4, 1, 6 * width))], axis=2)
    small = jnp.stack([small[0], small[2]]) + near(jnp.stack([small[1], small[3]]))
    small_sent = over_y(small[1])

    if lax.axis_size("dp") == 4:
        here = lax.axis_index("dp")
        middle = (here == 1) | (here == 2)
        (inward,), cross, (outward,) = chain_steps(4)
        totals = []
        mine[count] = small[0] + small_sent
        firsts_in, crossed = {}, {}
        for k in range(count + 1):
            prior = [crossed[k - 2]] if k >= 2 else []
            got = lax.ppermute(mine[k], "dp", inward)
            firsts_in[k] = after(mine[k], *prior) + got
            got = lax.ppermute(firsts_in[k], "dp", cross)
            crossed[k] = firsts_in[k] + got
            got = lax.ppermute(crossed[k], "dp", outward)
            totals.append(jnp.where(middle, crossed[k], got))
        small = totals.pop()
    else:
        totals = [chain_sum(mine[k], "dp") for k in range(count)]
        small = chain_sum(small[0] + small_sent, "dp")
    totals = [t.astype(F32) for t in totals]
    small = small[0]
    g_attn = jnp.concatenate(totals[4:6], axis=0).reshape(heads, -1, width).transpose(2, 0, 1)
    bias_sum = small[:cols].reshape(heads, 3, -1)
    grad_attn_bias = jnp.concatenate([bias_sum[:, 0], bias_sum[:, 2]], axis=1)
    rowed = small[cols + units:].reshape(6, 1, width)
    return (
        jnp.concatenate(outputs).reshape(1, micro, rows, width),
        jnp.concatenate([part[0] for part in attn_parts]).reshape(1, micro, rows, width),
        g_attn[None],
        grad_attn_bias[None],
        totals[6].reshape(proj_weight.shape),
        rowed[0],
        rowed[1],
        rowed[2],
        jnp.concatenate(totals[2:4], axis=0)[None],
        small[None, cols:cols + units],
        jnp.concatenate(totals[0:2], axis=0)[None],
        rowed[3],
        rowed[4],
        rowed[5],
    )


def solution(mesh):
    rows = P(None, ("dp", "tensor"), None)
    layer = P("section", None)
    placed = (
        rows, rows, P(None, "dp"), P(None, "dp", None),
        P("section", None, "tensor", None), P("section", "tensor", None), P("section", "tensor", None, None),
        layer, layer, layer, P("section", None, "tensor"), P("section", "tensor"), P("section", "tensor", None),
        layer, layer, layer,
    )
    both = P("section", None, ("dp", "tensor"), None)
    return jax.shard_map(
        body,
        mesh=mesh,
        in_specs=placed,
        out_specs=(both, both) + placed[4:],
        check_vma=False,
    )
```

```python
import functools

import jax
import jax.numpy as jnp
from jax import lax
from jax.experimental import pallas as pl
from jax.experimental.pallas import tpu as pltpu
from jax.sharding import PartitionSpec as P

HD = 64
SEQLEN = 208
norm_eps = 1e-06
masked_value = -1000000000.0
BF = jnp.bfloat16
F32 = jnp.float32
NT = (((1,), (1,)), ((), ()))
TN = (((0,), (0,)), ((), ()))
MIB = 1 << 20
PARTS = 3
EXTRA = 32


def dot(a, b):
    return jnp.dot(a, b, preferred_element_type=F32)


def dot_nt(a, b):
    return lax.dot_general(a, b, NT, preferred_element_type=F32)


def dot_tn(a, b):
    return lax.dot_general(a, b, TN, preferred_element_type=F32)


def normed(residual):
    center = residual - jnp.mean(residual, axis=-1, keepdims=True)
    rstd = lax.rsqrt(jnp.mean(center * center, axis=-1, keepdims=True) + norm_eps)
    return center * rstd, rstd


def norm_back(grad, n, rstd, gain):
    g = grad * gain
    return rstd * (g - jnp.mean(g, axis=-1, keepdims=True) - n * jnp.mean(g * n, axis=-1, keepdims=True))


def gelu_parts(u, slope):
    size = jnp.abs(u)
    t = pl.reciprocal(1.0 + 0.23164189 * size, approx=True)
    poly = t * (0.127414796 + t * (-0.142248368 + t * (0.7107068705 + t * (-0.7265760135 + t * 0.5307027145))))
    bell = jnp.exp2(u * (u * -0.7213475204444817))
    tail = poly * bell
    act = jnp.maximum(u, 0.0) - size * tail
    if not slope:
        return act, None
    return act, jnp.where(u < 0, tail, 1.0 - tail) + u * (bell * 0.3989422804014327)


def fixed(a):
    return pl.BlockSpec(a.shape, lambda q: (0,) * len(a.shape))


def quarter(a):
    return pl.BlockSpec((1,) + tuple(a.shape[1:]), lambda q: (q,) + (0,) * (len(a.shape) - 1))


def call(kernel, name, count, ins, outs, scratch, flops, limit=24):
    spec = lambda pair: (quarter if pair[1] else fixed)(pair[0])
    size = sum(a.size * a.dtype.itemsize for a, _ in (*ins, *outs))
    return pl.pallas_call(
        kernel,
        grid=(count,),
        in_specs=[spec(p) for p in ins],
        out_specs=[spec(p) for p in outs],
        out_shape=[a for a, _ in outs],
        scratch_shapes=scratch,
        compiler_params=pltpu.CompilerParams(vmem_limit_bytes=limit * MIB),
        cost_estimate=pl.CostEstimate(flops=1, bytes_accessed=1, transcendentals=0),
        name=name,
    )(*[a for a, _ in ins])


def shape(*dims, t=BF):
    return jax.ShapeDtypeStruct(dims, t)


def units_of(p, seqs):
    for s in range(seqs):
        for h in range(p.shape[1] // (3 * HD)):
            yield s, h


def head_rows(p, s, h, part):
    at = (3 * h + part) * HD
    return p[s * SEQLEN:(s + 1) * SEQLEN, at:at + HD]


def attn_fwd_kernel(save, first, seqs, x_ref, ok_ref, base_ref, ab_ref, wt_ref, pw_ref, r1_ref, *saved):
    q = pl.program_id(0)
    x = x_ref[...]

    @pl.when(q == 0)
    def _():
        r1_ref[...] = x.astype(F32) + base_ref[...] if first else base_ref[...]

    cols = ab_ref.shape[2]
    p = (dot_nt(x, wt_ref[0, :cols]) + ab_ref[0]).astype(BF)
    blocks = list(units_of(p, seqs))
    oks = [ok_ref[s] > 0 for s in range(seqs)]
    scores = [dot_nt(head_rows(p, s, h, 1), head_rows(p, s, h, 0) * 0.125) for s, h in blocks]
    probs = []
    for (s, h), st in zip(blocks, scores):
        st = jnp.where(oks[s], st, masked_value)
        e = jnp.exp(st - jnp.max(st, axis=0, keepdims=True))
        probs.append((e * (1.0 / jnp.sum(e, axis=0, keepdims=True))).astype(BF))
    cts = [dot_tn(head_rows(p, s, h, 2), a).astype(BF) for (s, h), a in zip(blocks, probs)]
    per = len(blocks) // seqs
    c = jnp.concatenate([jnp.concatenate(cts[s * per:(s + 1) * per], axis=0).T for s in range(seqs)], axis=0)
    r1_ref[...] += dot(c, pw_ref[0])
    if save:
        saved[0][0] = p
        saved[1][0] = c
        for (s, h), a in zip(blocks, probs):
            saved[2][0, s, h] = a


def attn_fwd(x, ok, base, ab, wt, pw, save, first):
    rows, width = x.shape
    count, _, cols = ab.shape
    seqs, heads = rows // SEQLEN, cols // (3 * HD)
    outs = [(shape(rows, width, t=F32), False)]
    if save:
        outs += [(shape(count, rows, cols), True), (shape(count, rows, heads * HD), True),
                 (shape(count, seqs, heads, SEQLEN, SEQLEN), True)]
    flops = count * 2 * rows * (width * cols + heads * HD * (2 * SEQLEN + width))
    ins = [(x, False), (ok, False), (base, False), (ab, True), (wt, True), (pw, True)]
    return call(functools.partial(attn_fwd_kernel, save, first, seqs), "attn_fwd", count, ins, outs, [], flops)


def ffn_fwd_kernel(save, first, last, x_ref, acc_in, vec_ref, ub_ref, up_ref, down_ref, *outs):
    q = pl.program_id(0)
    outs, (hb_ref, acc_ref) = outs[:-2], outs[-2:]

    @pl.when(q == 0)
    def _():
        if first:
            h = normed(x_ref[...])[0] * vec_ref[0:1] + vec_ref[1:2]
            hb_ref[...] = h.astype(BF)
            acc_ref[...] = h + vec_ref[2:3]
        else:
            hb_ref[...] = x_ref[...]
            acc_ref[...] = acc_in[...]

    hb = hb_ref[...]
    units = up_ref.shape[2]
    step = units // PARTS
    us = [dot(hb, up_ref[0, :, j * step:(j + 1) * step]) for j in range(PARTS)]
    es, slopes = [], []
    for j, u in enumerate(us):
        act, slope = gelu_parts(u + ub_ref[0, :, j * step:(j + 1) * step], save)
        es.append(act.astype(BF))
        if save:
            outs[2][0, :, j * step:(j + 1) * step] = slope.astype(BF)
    e = jnp.concatenate(es, axis=1)
    if save:
        outs[1][0] = e
    acc_ref[...] += dot(e, down_ref[0])

    @pl.when(q == pl.num_programs(0) - 1)
    def _():
        acc = acc_ref[...]
        if last:
            outs[0][...] = (normed(acc)[0] * vec_ref[3:4] + vec_ref[4:5]).astype(BF)
            if save:
                outs[3][...] = acc
                outs[4][...] = hb
        else:
            outs[0][...] = acc
            outs[1][...] = hb


def ffn_fwd(x, acc, vec, ub, up, down, save, first, last):
    rows, width = x.shape
    count, _, units = ub.shape
    outs = [(shape(rows, width, t=BF if last else F32), False)]
    if save:
        outs += [(shape(count, rows, units), True)] * 2 + [(shape(rows, width, t=F32), False), (shape(rows, width), False)]
    if not last:
        outs += [(shape(rows, width), False)]
    ins = [(x, False), (acc, False), (vec, False), (ub, True), (up, True), (down, True)]
    scratch = [pltpu.VMEM((rows, width), BF), pltpu.VMEM((rows, width), F32)]
    return call(functools.partial(ffn_fwd_kernel, save, first, last), "ffn_fwd", count, ins, outs, scratch,
                count * 4 * rows * width * units)


def ffn_bwd_kernel(full, dy_ref, r2_ref, r1_ref, vec_ref, slope_ref, up_ref, down_ref, *outs):
    q = pl.program_id(0)
    outs, (df_ref, dh_ref, sum_ref) = outs[:-3], outs[-3:]
    total = lambda v: jnp.sum(v, axis=0, keepdims=True)

    @pl.when(q == 0)
    def _():
        dy = dy_ref[...].astype(F32)
        n2, s2 = normed(r2_ref[...])
        dr2 = norm_back(dy, n2, s2, vec_ref[3:4])
        df_ref[...] = dr2.astype(BF)
        dh_ref[...] = dr2
        if full:
            sum_ref[0:1] = total(dr2)
            sum_ref[1:2] = total(dy * n2)
            sum_ref[2:3] = total(dy)

    df = df_ref[...]
    units = up_ref.shape[2]
    step = units // PARTS
    des = [dot_nt(df, down_ref[0, j * step:(j + 1) * step]) for j in range(PARTS)]
    dus = [(de * slope_ref[0, :, j * step:(j + 1) * step].astype(F32)).astype(BF) for j, de in enumerate(des)]
    du = jnp.concatenate(dus, axis=1)
    dh_ref[...] += dot_nt(du, up_ref[0])
    if full:
        outs[3][0] = du
        outs[4][0] = total(du.astype(F32))

    @pl.when(q == pl.num_programs(0) - 1)
    def _():
        dh = dh_ref[...]
        n1, s1 = normed(r1_ref[...])
        dr1 = norm_back(dh, n1, s1, vec_ref[0:1])
        outs[0][...] = dr1
        outs[1][...] = dr1.astype(BF)
        if full:
            outs[2][...] = df
            outs[5][0:1] = total(dr1)
            outs[5][1:2] = total(dh * n1)
            outs[5][2:3] = total(dh)
            outs[5][3:6] = sum_ref[0:3]
            outs[5][6:8] = jnp.zeros_like(outs[5][6:8])


def ffn_bwd(dy, r2, r1, vec, slope, up, down, full):
    rows, width = r1.shape
    count, _, units = slope.shape
    outs = [(shape(rows, width, t=F32), False), (shape(rows, width), False)]
    if full:
        outs += [(shape(rows, width), False), (shape(count, rows, units), True),
                 (shape(count, 1, units, t=F32), True), (shape(8, width, t=F32), False)]
    ins = [(dy, False), (r2, False), (r1, False), (vec, False), (slope, True), (up, True), (down, True)]
    scratch = [pltpu.VMEM((rows, width), BF), pltpu.VMEM((rows, width), F32), pltpu.VMEM((8, width), F32)]
    return call(functools.partial(ffn_bwd_kernel, full), "ffn_bwd", count, ins, outs, scratch,
                count * 4 * rows * width * units)


def attn_bwd_kernel(full, seqs, dg_ref, dr1_ref, p_ref, a_ref, wt_ref, pw_ref, *outs):
    q = pl.program_id(0)
    outs, dx_ref = outs[:-1], outs[-1]

    @pl.when(q == 0)
    def _():
        dx_ref[...] = dr1_ref[...]

    dc = dot_nt(dg_ref[...], pw_ref[0]).astype(BF)
    p = p_ref[0]
    blocks = list(units_of(p, seqs))
    dcs = [dc[s * SEQLEN:(s + 1) * SEQLEN, h * HD:(h + 1) * HD] for s, h in blocks]
    das = [dot_nt(head_rows(p, s, h, 2), d) for (s, h), d in zip(blocks, dcs)]
    dss = []
    for (s, h), da in zip(blocks, das):
        a = a_ref[0, s, h].astype(F32)
        dss.append((a * (da - jnp.sum(da * a, axis=0, keepdims=True))).astype(BF))
    pieces = []
    for (s, h), d, ds in zip(blocks, dcs, dss):
        dq = dot_tn(ds, head_rows(p, s, h, 1)) * 0.125
        dk = dot(ds, head_rows(p, s, h, 0)) * 0.125
        dv = dot(a_ref[0, s, h], d)
        pieces += [dq.astype(BF), dk.astype(BF), dv.astype(BF)]
    per = len(pieces) // seqs
    dp = jnp.concatenate([jnp.concatenate(pieces[s * per:(s + 1) * per], axis=1) for s in range(seqs)], axis=0)
    dx_ref[...] += dot(dp, wt_ref[0, :dp.shape[1]])
    if full:
        outs[1][0] = dp
        outs[2][0] = jnp.sum(dp.astype(F32), axis=0, keepdims=True)

    @pl.when(q == pl.num_programs(0) - 1)
    def _():
        outs[0][...] = dx_ref[...].astype(outs[0].dtype)


def attn_bwd(dg, dr1, p, a, wt, pw, full):
    rows, width = dg.shape
    count, _, cols = p.shape
    seqs, heads = rows // SEQLEN, cols // (3 * HD)
    outs = [(shape(rows, width, t=F32 if full else BF), False)]
    if full:
        outs += [(shape(count, rows, cols), True), (shape(count, 1, cols, t=F32), True)]
    ins = [(dg, False), (dr1, False), (p, True), (a, True), (wt, True), (pw, True)]
    flops = count * 2 * rows * (width * cols + heads * HD * (4 * SEQLEN + width))
    return call(functools.partial(attn_bwd_kernel, full, seqs), "attn_bwd", count, ins, outs,
                [pltpu.VMEM((rows, width), F32)], flops)


def wgrad_kernel(pairs, *refs):
    total = None
    for g in range(pairs):
        a, b = refs[2 * g], refs[2 * g + 1]
        a = a[0] if len(a.shape) == 3 else a[...]
        b = b[0] if len(b.shape) == 3 else b[...]
        part = dot_tn(a, b)
        total = part if total is None else total + part
    for more in refs[2 * pairs:-1]:
        total = total + more[0].astype(F32)
    refs[-1][0] = total.astype(BF)


def wgrad(pairs, odd, *more):
    def spec(a):
        if a.ndim == 2:
            return pl.BlockSpec(a.shape, lambda i: (0, 0))
        return pl.BlockSpec((1,) + a.shape[1:], lambda i: (2 * i + odd, 0, 0))

    flat = [a for pair in pairs for a in pair]
    dims = (2, pairs[0][0].shape[-1], pairs[0][1].shape[-1])
    block = pl.BlockSpec((1,) + dims[1:], lambda i: (i, 0, 0))
    return pl.pallas_call(
        functools.partial(wgrad_kernel, len(pairs)),
        grid=(2,),
        in_specs=[spec(a) for a in flat] + [block] * len(more),
        out_specs=block,
        out_shape=shape(*dims),
        compiler_params=pltpu.CompilerParams(vmem_limit_bytes=24 * MIB),
        cost_estimate=pl.CostEstimate(flops=1, bytes_accessed=1, transcendentals=0),
        name="wgrad",
    )(*flat, *more)


STEPS = (
    "out a", "out p", "take d", "held a", "held p", "cross d0", "in d1", "cross d1",
    "take u", "outw d0", "cross u0", "in u1", "outw d1", "fin d0", "take a", "cross u1",
    "outw u0", "cross a0", "in a1", "fin d1", "outw u1", "take s", "take p", "cross a1",
    "outw a0", "fin u0", "cross s0", "cross p0", "fin u1", "outw a1", "outw s0", "outw p0",
    "fin a0", "fin a1", "fin s0", "fin p0",
)


def swapped(value, axis, bit):
    count = lax.axis_size(axis)
    return lax.ppermute(value, axis, [(i, i ^ bit) for i in range(count)])


def near(value):
    return swapped(value, "tensor", 1)


def over_y(value):
    return swapped(value, "tensor", 2)


def chain_steps(count):
    half = count // 2
    inward = [[(s, s + 1), (count - 1 - s, count - 2 - s)] for s in range(half - 1)]
    outward = [[(s, s - 1), (count - 1 - s, count - s)] for s in range(half - 1, 0, -1)]
    return inward, [(half - 1, half), (half, half - 1)], outward


def chain_sum(value, axis):
    count = lax.axis_size(axis)
    if count == 1:
        return value
    if count % 2:
        return lax.psum(value, axis)
    here = lax.axis_index(axis)
    inward, cross, outward = chain_steps(count)
    for step in inward:
        value = value + lax.ppermute(value, axis, step)
    value = value + lax.ppermute(value, axis, cross)
    for step in outward:
        got = lax.ppermute(value, axis, step)
        takes = (here == step[0][1]) | (here == step[1][1])
        value = jnp.where(takes, got, value)
    return value


def after(value, *others):
    return lax.optimization_barrier((value, *others))[0]


def key_allowed(region_count, region_mask, caption):
    regions = region_mask.shape[-1]
    slot_index = jnp.arange(caption + regions, dtype=jnp.int32) - caption
    caption_ones = jnp.ones(region_mask.shape[:-1] + (caption,), jnp.int32)
    present = jnp.concatenate([caption_ones, region_mask], axis=-1) > 0
    return present & (slot_index < region_count[..., None])


def three_parts(vector):
    high = lax.reduce_precision(vector, 8, 7)
    mid = lax.reduce_precision(vector - high, 8, 7)
    return [high, mid, vector - high - mid]


def body(
    layer_input, cotangent, region_count, region_mask, attn_weight, attn_bias, proj_weight, proj_bias,
    first_gain, first_shift, up_weight, up_bias, down_weight, down_bias, second_gain, second_shift,
):
    section = lax.axis_index("section")
    tensor = lax.axis_index("tensor")
    micro, rows, width = layer_input.shape
    heads = attn_weight.shape[2]
    cols = heads * attn_weight.shape[3]
    units = up_weight.shape[2]
    assert rows == SEQLEN and lax.axis_size("tensor") == 4
    dp_pairs = lax.axis_size("dp") % 2 == 0
    odd = lax.axis_index("dp") % 2 == 1

    pieces = attn_bias[0].reshape(heads, 2, -1)
    own_bias = jnp.stack([pieces[:, 0], jnp.zeros_like(pieces[:, 0]), pieces[:, 1]], axis=1).reshape(-1)
    own_bias = jnp.pad(own_bias, (0, width - cols))
    tail = jnp.stack(three_parts(own_bias) + three_parts(up_bias[0])).astype(BF)
    tail = after(jnp.pad(tail, ((0, EXTRA - 6), (0, 0))))
    attn_own = attn_weight[0].transpose(1, 2, 0).reshape(cols, width)
    attn_own = jnp.concatenate([attn_own, tail], axis=0)
    proj_own = proj_weight[0].reshape(-1, width)
    up_own = up_weight[0]
    down_own = down_weight[0]

    def part(own):
        half = own.shape[0] // 2
        return jnp.where(odd, own[half:], own[:half]) if dp_pairs else own

    def along_dp(mine):
        return swapped(mine, "dp", 1) if dp_pairs else mine

    def both_halves(mine, pair):
        if not dp_pairs:
            return mine
        return jnp.where(odd, jnp.concatenate([pair, mine]), jnp.concatenate([mine, pair]))

    def pair_of(a, b):
        return jnp.stack([a, b])

    ok = lax.dynamic_index_in_dim(key_allowed(region_count, region_mask, rows - region_mask.shape[-1]), tensor, 1, False)
    ok = ok.astype(jnp.int32)[:, :, None]
    vec = jnp.concatenate([first_gain, first_shift, down_bias, second_gain, second_shift], axis=0)
    groups = 2 if micro % 2 == 0 else 1
    per = micro // groups
    size = per * rows
    cut = lambda value: [value.reshape(micro * rows, -1)[g * size:(g + 1) * size] for g in range(groups)]
    oks = [ok[g * per:(g + 1) * per] for g in range(groups)]
    x_own, cots = cut(layer_input), cut(cotangent)

    attn_mine = over_y(part(attn_own))
    attn_near = near(attn_own)
    proj_mine = over_y(part(proj_own))
    proj_near = near(proj_own)
    up_mine = over_y(after(part(up_own), attn_mine))
    attn_pair = along_dp(attn_mine)
    up_near = near(up_own)
    down_mine = over_y(after(part(down_own), proj_mine))
    proj_pair = along_dp(proj_mine)
    down_near = near(down_own)
    up_pair = along_dp(up_mine)
    down_pair = along_dp(down_mine)

    def biases(stack):
        three = stack[:, cols:cols + 6].astype(F32)
        return jnp.sum(three[:, :3], axis=1, keepdims=True)[:, :, :cols], jnp.sum(three[:, 3:], axis=1, keepdims=True)

    attn_0 = pair_of(attn_own, attn_near)
    proj_0 = pair_of(proj_own, proj_near)
    up_0 = pair_of(up_own, up_near)
    down_0 = pair_of(down_own, down_near)
    ab_0, ub_0 = biases(attn_0)
    r1s = [attn_fwd(x_own[g], oks[g], proj_bias, ab_0, attn_0, proj_0, False, True)[0] for g in range(groups)]
    attn_far = both_halves(attn_mine, attn_pair)
    attn_1 = pair_of(attn_far, near(attn_far))
    proj_far = both_halves(proj_mine, proj_pair)
    proj_1 = pair_of(proj_far, near(proj_far))
    ab_1, ub_1 = biases(attn_1)
    r1s = [attn_fwd(x_own[g], oks[g], r1s[g], ab_1, attn_1, proj_1, False, False)[0] for g in range(groups)]
    halves = [ffn_fwd(r1s[g], vec, vec, ub_0, up_0, down_0, False, True, False) for g in range(groups)]
    up_far = both_halves(up_mine, up_pair)
    up_1 = pair_of(up_far, near(up_far))
    down_far = both_halves(down_mine, down_pair)
    down_1 = pair_of(down_far, near(down_far))
    firsts, hops = [], []
    for g in range(groups):
        tok = firsts[-1:]
        acc, hb = halves[g]
        firsts.append(ffn_fwd(hb, after(acc, *tok), vec, ub_1, up_1, down_1, False, False, True)[0])
        hops.append(lax.ppermute(after(firsts[g], *hops[-1:]), "section", [(0, 1)]))

    tok = firsts[-1]
    attn_w = jnp.concatenate([after(attn_0, tok), attn_1])
    proj_w = jnp.concatenate([after(proj_0, tok), proj_1])
    up_w = jnp.concatenate([after(up_0, tok), up_1])
    down_w = jnp.concatenate([after(down_0, tok), down_1])
    ab = jnp.concatenate([ab_0, ab_1])
    ub = jnp.concatenate([ub_0, ub_1])

    kept, outputs, backs = [], [], []
    tok = (up_w, down_w)
    for g in range(groups):
        x = jnp.where(section == 0, after(x_own[g], *tok), hops[g])
        r1, p, c, a = attn_fwd(x, oks[g], proj_bias, ab, attn_w, proj_w, True, True)
        y, e, slope, r2, hb = ffn_fwd(r1, vec, vec, ub, up_w, down_w, True, True, True)
        dr1, dg = ffn_bwd(cots[g], r2, r1, vec, slope, up_w, down_w, False)
        (d_first,) = attn_bwd(dg, dr1, p, a, attn_w, proj_w, False)
        backs.append(lax.ppermute(d_first, "section", [(1, 0)]))
        kept.append((x, r1, p, c, a, e, slope, r2, hb))
        outputs.append(y)
        tok = (d_first,)

    def ffn_part(g, *before):
        x, r1, p, c, a, e, slope, r2, hb = kept[g]
        dy = jnp.where(section == 1, after(cots[g], *before), backs[g])
        return ffn_bwd(dy, r2, r1, vec, slope, up_w, down_w, True)

    def attn_part(g, dg, dr1):
        x, r1, p, c, a, e, slope, r2, hb = kept[g]
        return attn_bwd(dg, dr1, p, a, attn_w, proj_w, True)

    ffn_parts, attn_parts = [], []
    down_pre, up_pre = [[], []], [[], []]

    def following(terms, *before):
        return [(after(terms[0][0], *before), terms[0][1])] + terms[1:]

    for g in range(groups):
        ffn_parts.append(ffn_part(g, *tok))
        if g < groups - 1:
            down_term = (kept[g][5], ffn_parts[g][2])
            up_term = (kept[g][8], ffn_parts[g][3])
            for odd_share in (1, 0):
                down_pre[odd_share] = [wgrad([down_term], odd_share, *down_pre[odd_share])]
                up_pre[odd_share] = [wgrad([up_term], odd_share, *up_pre[odd_share])]
            tok = (*down_pre[0], *down_pre[1], *up_pre[0], *up_pre[1])
    g = groups - 1
    down_terms, up_terms = [(kept[g][5], ffn_parts[g][2])], [(kept[g][8], ffn_parts[g][3])]
    all_of = lambda a, b: [(a(g), b(g)) for g in range(groups)]
    proj_terms = all_of(lambda g: kept[g][3], lambda g: ffn_parts[g][1])

    out_d = wgrad(down_terms, 1, *down_pre[1])
    got_d = near(out_d)
    out_u = wgrad(following(up_terms, out_d), 1, *up_pre[1])
    got_u = near(out_u)
    held_d = wgrad(following(down_terms, out_u), 0, *down_pre[0], got_d)
    held_u = wgrad(following(up_terms, held_d), 0, *up_pre[0], got_u)
    tok = (held_u,)
    for g in range(groups):
        attn_parts.append(attn_part(g, after(ffn_parts[g][1], *tok), ffn_parts[g][0]))
        tok = (attn_parts[g][0],)
    attn_terms = all_of(lambda g: attn_parts[g][1], lambda g: kept[g][0])
    half, half_u, half_a = units // 2, width // 2, cols // 2

    bias_sums = sum(part[2] for part in attn_parts)
    unit_sums = sum(part[4] for part in ffn_parts)
    row_sums = sum(part[5] for part in ffn_parts)[:6].reshape(1, 1, -1)
    small = jnp.concatenate([bias_sums, unit_sums, jnp.broadcast_to(row_sums, (4, 1, 6 * width))], axis=2)
    small = jnp.stack([small[0], small[2]]) + near(jnp.stack([small[1], small[3]]))
    count_of = {"d": 2, "u": 2, "a": 2, "p": 1, "s": 1}
    helds = {"d": held_d, "u": held_u, "s": small}
    sent = {"d": over_y(held_d[1]), "u": over_y(held_u[1]), "s": over_y(small[1])}
    chain = lax.axis_size("dp") == 4
    middle = (lax.axis_index("dp") == 1) | (lax.axis_index("dp") == 2)
    inward, cross, outward = chain_steps(lax.axis_size("dp")) if chain else (None, None, None)
    tok = (attn_parts[-1][0],)
    mine, got, totals = {}, {}, {}
    for step in STEPS:
        what, key = step.split()
        if what == "out":
            terms = {"a": attn_terms, "p": proj_terms}[key]
            share = wgrad(following(terms, *tok), 1)
            got[key] = near(share)
            tok = (share,)
        elif what == "held":
            terms = {"a": attn_terms, "p": proj_terms}[key]
            helds[key] = wgrad(following(terms, *tok), 0, got[key])
            sent[key] = over_y(helds[key][1])
            tok = (helds[key],)
        elif what == "take":
            held = after(helds[key], *tok)
            part = held.shape[1] // count_of[key]
            for i in range(count_of[key]):
                k = key + str(i)
                mine[k] = held[0, i * part:(i + 1) * part] + sent[key][i * part:(i + 1) * part]
                tok = (mine[k],)
                if chain and "in " + k not in STEPS:
                    got[k] = lax.ppermute(mine[k], "dp", inward[0])
                elif not chain:
                    totals[k] = chain_sum(mine[k], "dp")
        elif not chain:
            continue
        elif what == "in":
            got[key] = lax.ppermute(after(mine[key], *tok), "dp", inward[0])
        elif what == "fin":
            totals[key] = jnp.where(middle, after(mine[key], *tok), got[key])
            tok = (totals[key],)
        else:
            mine[key] = after(mine[key], *tok) + got[key]
            tok = (mine[key],)
            got[key] = lax.ppermute(mine[key], "dp", cross if what == "cross" else outward[0])
    small = totals["s0"]
    totals = [totals[k] for k in ("d0", "d1", "u0", "u1", "a0", "a1", "p0")]
    totals = [t.astype(F32) for t in totals]
    small = small[0]
    g_attn = jnp.concatenate(totals[4:6], axis=0).reshape(heads, -1, width).transpose(2, 0, 1)
    bias_sum = small[:cols].reshape(heads, 3, -1)
    grad_attn_bias = jnp.concatenate([bias_sum[:, 0], bias_sum[:, 2]], axis=1)
    rowed = small[cols + units:].reshape(6, 1, width)
    return (
        jnp.concatenate(outputs).reshape(1, micro, rows, width),
        jnp.concatenate([part[0] for part in attn_parts]).reshape(1, micro, rows, width),
        g_attn[None],
        grad_attn_bias[None],
        totals[6].reshape(proj_weight.shape),
        rowed[0],
        rowed[1],
        rowed[2],
        jnp.concatenate(totals[2:4], axis=0)[None],
        small[None, cols:cols + units],
        jnp.concatenate(totals[:2], axis=0)[None],
        rowed[3],
        rowed[4],
        rowed[5],
    )


def solution(mesh):
    rows = P(None, ("dp", "tensor"), None)
    layer = P("section", None)
    placed = (
        rows, rows, P(None, "dp"), P(None, "dp", None),
        P("section", None, "tensor", None), P("section", "tensor", None), P("section", "tensor", None, None),
        layer, layer, layer, P("section", None, "tensor"), P("section", "tensor"), P("section", "tensor", None),
        layer, layer, layer,
    )
    both = P("section", None, ("dp", "tensor"), None)
    return jax.shard_map(
        body,
        mesh=mesh,
        in_specs=placed,
        out_specs=(both, both) + placed[4:],
        check_vma=False,
    )
```

```python
import functools

import jax
import jax.numpy as jnp
from jax import lax
from jax.experimental import pallas as pl
from jax.experimental.pallas import tpu as pltpu
from jax.sharding import PartitionSpec as P

HD = 64
SEQLEN = 208
norm_eps = 1e-06
masked_value = -1000000000.0
BF = jnp.bfloat16
F32 = jnp.float32
NT = (((1,), (1,)), ((), ()))
TN = (((0,), (0,)), ((), ()))
MIB = 1 << 20
PARTS = 3
EXTRA = 32


def dot(a, b):
    return jnp.dot(a, b, preferred_element_type=F32)


def dot_nt(a, b):
    return lax.dot_general(a, b, NT, preferred_element_type=F32)


def dot_tn(a, b):
    return lax.dot_general(a, b, TN, preferred_element_type=F32)


def normed(residual):
    center = residual - jnp.mean(residual, axis=-1, keepdims=True)
    rstd = lax.rsqrt(jnp.mean(center * center, axis=-1, keepdims=True) + norm_eps)
    return center * rstd, rstd


def norm_back(grad, n, rstd, gain):
    g = grad * gain
    return rstd * (g - jnp.mean(g, axis=-1, keepdims=True) - n * jnp.mean(g * n, axis=-1, keepdims=True))


def gelu_parts(u, slope):
    size = jnp.abs(u)
    t = pl.reciprocal(1.0 + 0.23164189 * size, approx=True)
    poly = t * (0.127414796 + t * (-0.142248368 + t * (0.7107068705 + t * (-0.7265760135 + t * 0.5307027145))))
    bell = jnp.exp2(u * (u * -0.7213475204444817))
    tail = poly * bell
    act = jnp.maximum(u, 0.0) - size * tail
    if not slope:
        return act, None
    return act, jnp.where(u < 0, tail, 1.0 - tail) + u * (bell * 0.3989422804014327)


def fixed(a):
    return pl.BlockSpec(a.shape, lambda q: (0,) * len(a.shape))


def quarter(a):
    return pl.BlockSpec((1,) + tuple(a.shape[1:]), lambda q: (q,) + (0,) * (len(a.shape) - 1))


def call(kernel, name, count, ins, outs, scratch, flops, limit=24):
    spec = lambda pair: (quarter if pair[1] else fixed)(pair[0])
    size = sum(a.size * a.dtype.itemsize for a, _ in (*ins, *outs))
    return pl.pallas_call(
        kernel,
        grid=(count,),
        in_specs=[spec(p) for p in ins],
        out_specs=[spec(p) for p in outs],
        out_shape=[a for a, _ in outs],
        scratch_shapes=scratch,
        compiler_params=pltpu.CompilerParams(vmem_limit_bytes=limit * MIB),
        cost_estimate=pl.CostEstimate(flops=1, bytes_accessed=1, transcendentals=0),
        name=name,
    )(*[a for a, _ in ins])


def shape(*dims, t=BF):
    return jax.ShapeDtypeStruct(dims, t)


def units_of(p, seqs):
    for s in range(seqs):
        for h in range(p.shape[1] // (3 * HD)):
            yield s, h


def head_rows(p, s, h, part):
    at = (3 * h + part) * HD
    return p[s * SEQLEN:(s + 1) * SEQLEN, at:at + HD]


def attn_fwd_kernel(save, first, seqs, x_ref, ok_ref, base_ref, ab_ref, wt_ref, pw_ref, r1_ref, *saved):
    q = pl.program_id(0)
    x = x_ref[...]

    @pl.when(q == 0)
    def _():
        r1_ref[...] = x.astype(F32) + base_ref[...] if first else base_ref[...]

    cols = ab_ref.shape[2]
    p = (dot_nt(x, wt_ref[0, :cols]) + ab_ref[0]).astype(BF)
    blocks = list(units_of(p, seqs))
    oks = [ok_ref[s] > 0 for s in range(seqs)]
    scores = [dot_nt(head_rows(p, s, h, 1), head_rows(p, s, h, 0) * 0.125) for s, h in blocks]
    probs = []
    for (s, h), st in zip(blocks, scores):
        st = jnp.where(oks[s], st, masked_value)
        e = jnp.exp(st - jnp.max(st, axis=0, keepdims=True))
        probs.append((e * (1.0 / jnp.sum(e, axis=0, keepdims=True))).astype(BF))
    cts = [dot_tn(head_rows(p, s, h, 2), a).astype(BF) for (s, h), a in zip(blocks, probs)]
    per = len(blocks) // seqs
    c = jnp.concatenate([jnp.concatenate(cts[s * per:(s + 1) * per], axis=0).T for s in range(seqs)], axis=0)
    r1_ref[...] += dot(c, pw_ref[0])
    if save:
        saved[0][0] = p
        saved[1][0] = c
        for (s, h), a in zip(blocks, probs):
            saved[2][0, s, h] = a


def attn_fwd(x, ok, base, ab, wt, pw, save, first):
    rows, width = x.shape
    count, _, cols = ab.shape
    seqs, heads = rows // SEQLEN, cols // (3 * HD)
    outs = [(shape(rows, width, t=F32), False)]
    if save:
        outs += [(shape(count, rows, cols), True), (shape(count, rows, heads * HD), True),
                 (shape(count, seqs, heads, SEQLEN, SEQLEN), True)]
    flops = count * 2 * rows * (width * cols + heads * HD * (2 * SEQLEN + width))
    ins = [(x, False), (ok, False), (base, False), (ab, True), (wt, True), (pw, True)]
    return call(functools.partial(attn_fwd_kernel, save, first, seqs), "attn_fwd", count, ins, outs, [], flops)


def ffn_fwd_kernel(save, first, last, x_ref, acc_in, vec_ref, ub_ref, up_ref, down_ref, *outs):
    q = pl.program_id(0)
    outs, (hb_ref, acc_ref) = outs[:-2], outs[-2:]

    @pl.when(q == 0)
    def _():
        if first:
            h = normed(x_ref[...])[0] * vec_ref[0:1] + vec_ref[1:2]
            hb_ref[...] = h.astype(BF)
            acc_ref[...] = h + vec_ref[2:3]
        else:
            hb_ref[...] = x_ref[...]
            acc_ref[...] = acc_in[...]

    hb = hb_ref[...]
    units = up_ref.shape[2]
    pieces = 2
    step = units // pieces
    us = [dot(hb, up_ref[0, :, j * step:(j + 1) * step]) for j in range(pieces)]
    es, slopes = [], []
    for j, u in enumerate(us):
        act, slope = gelu_parts(u + ub_ref[0, :, j * step:(j + 1) * step], save)
        es.append(act.astype(BF))
        if save:
            outs[2][0, :, j * step:(j + 1) * step] = slope.astype(BF)
    e = jnp.concatenate(es, axis=1)
    if save:
        outs[1][0] = e
    acc_ref[...] += dot(e, down_ref[0])

    @pl.when(q == pl.num_programs(0) - 1)
    def _():
        acc = acc_ref[...]
        if last:
            outs[0][...] = (normed(acc)[0] * vec_ref[3:4] + vec_ref[4:5]).astype(BF)
            if save:
                outs[3][...] = acc
                outs[4][...] = hb
        else:
            outs[0][...] = acc
            outs[1][...] = hb


def ffn_fwd(x, acc, vec, ub, up, down, save, first, last):
    rows, width = x.shape
    count, _, units = ub.shape
    outs = [(shape(rows, width, t=BF if last else F32), False)]
    if save:
        outs += [(shape(count, rows, units), True)] * 2 + [(shape(rows, width, t=F32), False), (shape(rows, width), False)]
    if not last:
        outs += [(shape(rows, width), False)]
    ins = [(x, False), (acc, False), (vec, False), (ub, True), (up, True), (down, True)]
    scratch = [pltpu.VMEM((rows, width), BF), pltpu.VMEM((rows, width), F32)]
    return call(functools.partial(ffn_fwd_kernel, save, first, last), "ffn_fwd", count, ins, outs, scratch,
                count * 4 * rows * width * units)


def ffn_bwd_kernel(full, dy_ref, r2_ref, r1_ref, vec_ref, slope_ref, up_ref, down_ref, *outs):
    q = pl.program_id(0)
    outs, (df_ref, dh_ref, sum_ref) = outs[:-3], outs[-3:]
    total = lambda v: jnp.sum(v, axis=0, keepdims=True)

    @pl.when(q == 0)
    def _():
        dy = dy_ref[...].astype(F32)
        n2, s2 = normed(r2_ref[...])
        dr2 = norm_back(dy, n2, s2, vec_ref[3:4])
        df_ref[...] = dr2.astype(BF)
        dh_ref[...] = dr2
        if full:
            sum_ref[0:1] = total(dr2)
            sum_ref[1:2] = total(dy * n2)
            sum_ref[2:3] = total(dy)

    df = df_ref[...]
    units = up_ref.shape[2]
    step = units // PARTS
    des = [dot_nt(df, down_ref[0, j * step:(j + 1) * step]) for j in range(PARTS)]
    dus = [(de * slope_ref[0, :, j * step:(j + 1) * step].astype(F32)).astype(BF) for j, de in enumerate(des)]
    du = jnp.concatenate(dus, axis=1)
    dh_ref[...] += dot_nt(du, up_ref[0])
    if full:
        outs[3][0] = du
        outs[4][0] = total(du.astype(F32))

    @pl.when(q == pl.num_programs(0) - 1)
    def _():
        dh = dh_ref[...]
        n1, s1 = normed(r1_ref[...])
        dr1 = norm_back(dh, n1, s1, vec_ref[0:1])
        outs[0][...] = dr1
        outs[1][...] = dr1.astype(BF)
        if full:
            outs[2][...] = df
            outs[5][0:1] = total(dr1)
            outs[5][1:2] = total(dh * n1)
            outs[5][2:3] = total(dh)
            outs[5][3:6] = sum_ref[0:3]
            outs[5][6:8] = jnp.zeros_like(outs[5][6:8])


def ffn_bwd(dy, r2, r1, vec, slope, up, down, full):
    rows, width = r1.shape
    count, _, units = slope.shape
    outs = [(shape(rows, width, t=F32), False), (shape(rows, width), False)]
    if full:
        outs += [(shape(rows, width), False), (shape(count, rows, units), True),
                 (shape(count, 1, units, t=F32), True), (shape(8, width, t=F32), False)]
    ins = [(dy, False), (r2, False), (r1, False), (vec, False), (slope, True), (up, True), (down, True)]
    scratch = [pltpu.VMEM((rows, width), BF), pltpu.VMEM((rows, width), F32), pltpu.VMEM((8, width), F32)]
    return call(functools.partial(ffn_bwd_kernel, full), "ffn_bwd", count, ins, outs, scratch,
                count * 4 * rows * width * units)


def attn_bwd_kernel(full, seqs, dg_ref, dr1_ref, p_ref, a_ref, wt_ref, pw_ref, *outs):
    q = pl.program_id(0)
    outs, dx_ref = outs[:-1], outs[-1]

    @pl.when(q == 0)
    def _():
        dx_ref[...] = dr1_ref[...]

    dc = dot_nt(dg_ref[...], pw_ref[0]).astype(BF)
    p = p_ref[0]
    blocks = list(units_of(p, seqs))
    dcs = [dc[s * SEQLEN:(s + 1) * SEQLEN, h * HD:(h + 1) * HD] for s, h in blocks]
    das = [dot_nt(head_rows(p, s, h, 2), d) for (s, h), d in zip(blocks, dcs)]
    dss = []
    for (s, h), da in zip(blocks, das):
        a = a_ref[0, s, h].astype(F32)
        dss.append((a * (da - jnp.sum(da * a, axis=0, keepdims=True))).astype(BF))
    pieces = []
    for (s, h), d, ds in zip(blocks, dcs, dss):
        dq = dot_tn(ds, head_rows(p, s, h, 1)) * 0.125
        dk = dot(ds, head_rows(p, s, h, 0)) * 0.125
        dv = dot(a_ref[0, s, h], d)
        pieces += [dq.astype(BF), dk.astype(BF), dv.astype(BF)]
    per = len(pieces) // seqs
    dp = jnp.concatenate([jnp.concatenate(pieces[s * per:(s + 1) * per], axis=1) for s in range(seqs)], axis=0)
    dx_ref[...] += dot(dp, wt_ref[0, :dp.shape[1]])
    if full:
        outs[1][0] = dp
        outs[2][0] = jnp.sum(dp.astype(F32), axis=0, keepdims=True)

    @pl.when(q == pl.num_programs(0) - 1)
    def _():
        outs[0][...] = dx_ref[...].astype(outs[0].dtype)


def attn_bwd(dg, dr1, p, a, wt, pw, full):
    rows, width = dg.shape
    count, _, cols = p.shape
    seqs, heads = rows // SEQLEN, cols // (3 * HD)
    outs = [(shape(rows, width, t=F32 if full else BF), False)]
    if full:
        outs += [(shape(count, rows, cols), True), (shape(count, 1, cols, t=F32), True)]
    ins = [(dg, False), (dr1, False), (p, True), (a, True), (wt, True), (pw, True)]
    flops = count * 2 * rows * (width * cols + heads * HD * (4 * SEQLEN + width))
    return call(functools.partial(attn_bwd_kernel, full, seqs), "attn_bwd", count, ins, outs,
                [pltpu.VMEM((rows, width), F32)], flops)


def wgrad_kernel(pairs, *refs):
    total = None
    for g in range(pairs):
        a, b = refs[2 * g], refs[2 * g + 1]
        a = a[0] if len(a.shape) == 3 else a[...]
        b = b[0] if len(b.shape) == 3 else b[...]
        part = dot_tn(a, b)
        total = part if total is None else total + part
    for more in refs[2 * pairs:-1]:
        total = total + more[0].astype(F32)
    refs[-1][0] = total.astype(BF)


def wgrad(pairs, odd, *more):
    def spec(a):
        if a.ndim == 2:
            return pl.BlockSpec(a.shape, lambda i: (0, 0))
        return pl.BlockSpec((1,) + a.shape[1:], lambda i: (2 * i + odd, 0, 0))

    flat = [a for pair in pairs for a in pair]
    dims = (2, pairs[0][0].shape[-1], pairs[0][1].shape[-1])
    block = pl.BlockSpec((1,) + dims[1:], lambda i: (i, 0, 0))
    return pl.pallas_call(
        functools.partial(wgrad_kernel, len(pairs)),
        grid=(2,),
        in_specs=[spec(a) for a in flat] + [block] * len(more),
        out_specs=block,
        out_shape=shape(*dims),
        compiler_params=pltpu.CompilerParams(vmem_limit_bytes=24 * MIB),
        cost_estimate=pl.CostEstimate(flops=1, bytes_accessed=1, transcendentals=0),
        name="wgrad",
    )(*flat, *more)


STEPS = (
    "out a", "out p", "take d", "held a", "held p", "cross d0", "in d1", "cross d1",
    "take u", "outw d0", "cross u0", "in u1", "outw d1", "fin d0", "take a", "cross u1",
    "outw u0", "cross a0", "in a1", "fin d1", "outw u1", "take s", "take p", "cross a1",
    "outw a0", "fin u0", "cross s0", "cross p0", "fin u1", "outw a1", "outw s0", "outw p0",
    "fin a0", "fin a1", "fin s0", "fin p0",
)


def swapped(value, axis, bit):
    count = lax.axis_size(axis)
    return lax.ppermute(value, axis, [(i, i ^ bit) for i in range(count)])


def near(value):
    return swapped(value, "tensor", 1)


def over_y(value):
    return swapped(value, "tensor", 2)


def chain_steps(count):
    half = count // 2
    inward = [[(s, s + 1), (count - 1 - s, count - 2 - s)] for s in range(half - 1)]
    outward = [[(s, s - 1), (count - 1 - s, count - s)] for s in range(half - 1, 0, -1)]
    return inward, [(half - 1, half), (half, half - 1)], outward


def chain_sum(value, axis):
    count = lax.axis_size(axis)
    if count == 1:
        return value
    if count % 2:
        return lax.psum(value, axis)
    here = lax.axis_index(axis)
    inward, cross, outward = chain_steps(count)
    for step in inward:
        value = value + lax.ppermute(value, axis, step)
    value = value + lax.ppermute(value, axis, cross)
    for step in outward:
        got = lax.ppermute(value, axis, step)
        takes = (here == step[0][1]) | (here == step[1][1])
        value = jnp.where(takes, got, value)
    return value


def after(value, *others):
    return lax.optimization_barrier((value, *others))[0]


def key_allowed(region_count, region_mask, caption):
    regions = region_mask.shape[-1]
    slot_index = jnp.arange(caption + regions, dtype=jnp.int32) - caption
    caption_ones = jnp.ones(region_mask.shape[:-1] + (caption,), jnp.int32)
    present = jnp.concatenate([caption_ones, region_mask], axis=-1) > 0
    return present & (slot_index < region_count[..., None])


def three_parts(vector):
    high = lax.reduce_precision(vector, 8, 7)
    mid = lax.reduce_precision(vector - high, 8, 7)
    return [high, mid, vector - high - mid]


def body(
    layer_input, cotangent, region_count, region_mask, attn_weight, attn_bias, proj_weight, proj_bias,
    first_gain, first_shift, up_weight, up_bias, down_weight, down_bias, second_gain, second_shift,
):
    section = lax.axis_index("section")
    tensor = lax.axis_index("tensor")
    micro, rows, width = layer_input.shape
    heads = attn_weight.shape[2]
    cols = heads * attn_weight.shape[3]
    units = up_weight.shape[2]
    assert rows == SEQLEN and lax.axis_size("tensor") == 4
    dp_pairs = lax.axis_size("dp") % 2 == 0
    odd = lax.axis_index("dp") % 2 == 1

    pieces = attn_bias[0].reshape(heads, 2, -1)
    own_bias = jnp.stack([pieces[:, 0], jnp.zeros_like(pieces[:, 0]), pieces[:, 1]], axis=1).reshape(-1)
    own_bias = jnp.pad(own_bias, (0, width - cols))
    tail = jnp.stack(three_parts(own_bias) + three_parts(up_bias[0])).astype(BF)
    tail = after(jnp.pad(tail, ((0, EXTRA - 6), (0, 0))))
    attn_own = attn_weight[0].transpose(1, 2, 0).reshape(cols, width)
    attn_own = jnp.concatenate([attn_own, tail], axis=0)
    proj_own = proj_weight[0].reshape(-1, width)
    up_own = up_weight[0]
    down_own = down_weight[0]

    def part(own):
        half = own.shape[0] // 2
        return jnp.where(odd, own[half:], own[:half]) if dp_pairs else own

    def along_dp(mine):
        return swapped(mine, "dp", 1) if dp_pairs else mine

    def both_halves(mine, pair):
        if not dp_pairs:
            return mine
        return jnp.where(odd, jnp.concatenate([pair, mine]), jnp.concatenate([mine, pair]))

    def pair_of(a, b):
        return jnp.stack([a, b])

    ok = lax.dynamic_index_in_dim(key_allowed(region_count, region_mask, rows - region_mask.shape[-1]), tensor, 1, False)
    ok = ok.astype(jnp.int32)[:, :, None]
    vec = jnp.concatenate([first_gain, first_shift, down_bias, second_gain, second_shift], axis=0)
    groups = 2 if micro % 2 == 0 else 1
    per = micro // groups
    size = per * rows
    cut = lambda value: [value.reshape(micro * rows, -1)[g * size:(g + 1) * size] for g in range(groups)]
    oks = [ok[g * per:(g + 1) * per] for g in range(groups)]
    x_own, cots = cut(layer_input), cut(cotangent)

    attn_mine = over_y(part(attn_own))
    attn_near = near(attn_own)
    proj_mine = over_y(part(proj_own))
    proj_near = near(proj_own)
    up_mine = over_y(after(part(up_own), attn_mine))
    attn_pair = along_dp(attn_mine)
    up_near = near(up_own)
    down_mine = over_y(after(part(down_own), proj_mine))
    proj_pair = along_dp(proj_mine)
    down_near = near(down_own)
    up_pair = along_dp(up_mine)
    down_pair = along_dp(down_mine)

    def biases(stack):
        three = stack[:, cols:cols + 6].astype(F32)
        return jnp.sum(three[:, :3], axis=1, keepdims=True)[:, :, :cols], jnp.sum(three[:, 3:], axis=1, keepdims=True)

    attn_0 = pair_of(attn_own, attn_near)
    proj_0 = pair_of(proj_own, proj_near)
    up_0 = pair_of(up_own, up_near)
    down_0 = pair_of(down_own, down_near)
    ab_0, ub_0 = biases(attn_0)
    r1s = [attn_fwd(x_own[g], oks[g], proj_bias, ab_0, attn_0, proj_0, False, True)[0] for g in range(groups)]
    attn_far = both_halves(attn_mine, attn_pair)
    attn_1 = pair_of(attn_far, near(attn_far))
    proj_far = both_halves(proj_mine, proj_pair)
    proj_1 = pair_of(proj_far, near(proj_far))
    ab_1, ub_1 = biases(attn_1)
    r1s = [attn_fwd(x_own[g], oks[g], r1s[g], ab_1, attn_1, proj_1, False, False)[0] for g in range(groups)]
    halves = [ffn_fwd(r1s[g], vec, vec, ub_0, up_0, down_0, False, True, False) for g in range(groups)]
    up_far = both_halves(up_mine, up_pair)
    up_1 = pair_of(up_far, near(up_far))
    down_far = both_halves(down_mine, down_pair)
    down_1 = pair_of(down_far, near(down_far))
    firsts, hops = [], []
    for g in range(groups):
        tok = firsts[-1:]
        acc, hb = halves[g]
        firsts.append(ffn_fwd(hb, after(acc, *tok), vec, ub_1, up_1, down_1, False, False, True)[0])
        hops.append(swapped(after(firsts[g], *hops[-1:]), "section", 1))

    tok = firsts[-1]
    attn_w = jnp.concatenate([after(attn_0, tok), attn_1])
    proj_w = jnp.concatenate([after(proj_0, tok), proj_1])
    up_w = jnp.concatenate([after(up_0, tok), up_1])
    down_w = jnp.concatenate([after(down_0, tok), down_1])
    ab = jnp.concatenate([ab_0, ab_1])
    ub = jnp.concatenate([ub_0, ub_1])

    kept, outputs, backs = [], [], []
    tok = (up_w, down_w)
    for g in range(groups):
        x = jnp.where(section == 0, after(x_own[g], *tok), hops[g])
        r1, p, c, a = attn_fwd(x, oks[g], proj_bias, ab, attn_w, proj_w, True, True)
        y, e, slope, r2, hb = ffn_fwd(r1, vec, vec, ub, up_w, down_w, True, True, True)
        dr1, dg = ffn_bwd(cots[g], r2, r1, vec, slope, up_w, down_w, False)
        (d_first,) = attn_bwd(dg, dr1, p, a, attn_w, proj_w, False)
        backs.append(swapped(d_first, "section", 1))
        kept.append((x, r1, p, c, a, e, slope, r2, hb))
        outputs.append(y)
        tok = (d_first,)

    def ffn_part(g, *before):
        x, r1, p, c, a, e, slope, r2, hb = kept[g]
        dy = jnp.where(section == 1, after(cots[g], *before), backs[g])
        return ffn_bwd(dy, r2, r1, vec, slope, up_w, down_w, True)

    def attn_part(g, dg, dr1):
        x, r1, p, c, a, e, slope, r2, hb = kept[g]
        return attn_bwd(dg, dr1, p, a, attn_w, proj_w, True)

    ffn_parts, attn_parts = [], []
    down_pre, up_pre = [[], []], [[], []]

    def following(terms, *before):
        return [(after(terms[0][0], *before), terms[0][1])] + terms[1:]

    for g in range(groups):
        ffn_parts.append(ffn_part(g, *tok))
        if g < groups - 1:
            down_term = (kept[g][5], ffn_parts[g][2])
            up_term = (kept[g][8], ffn_parts[g][3])
            for odd_share in (1, 0):
                down_pre[odd_share] = [wgrad([down_term], odd_share, *down_pre[odd_share])]
                up_pre[odd_share] = [wgrad([up_term], odd_share, *up_pre[odd_share])]
            tok = (*down_pre[0], *down_pre[1], *up_pre[0], *up_pre[1])
    g = groups - 1
    down_terms, up_terms = [(kept[g][5], ffn_parts[g][2])], [(kept[g][8], ffn_parts[g][3])]
    all_of = lambda a, b: [(a(g), b(g)) for g in range(groups)]
    proj_terms = all_of(lambda g: kept[g][3], lambda g: ffn_parts[g][1])

    out_d = wgrad(down_terms, 1, *down_pre[1])
    got_d = near(out_d)
    out_u = wgrad(following(up_terms, out_d), 1, *up_pre[1])
    got_u = near(out_u)
    held_d = wgrad(following(down_terms, out_u), 0, *down_pre[0], got_d)
    held_u = wgrad(following(up_terms, held_d), 0, *up_pre[0], got_u)
    tok = (held_u,)
    for g in range(groups):
        attn_parts.append(attn_part(g, after(ffn_parts[g][1], *tok), ffn_parts[g][0]))
        tok = (attn_parts[g][0],)
    attn_terms = all_of(lambda g: attn_parts[g][1], lambda g: kept[g][0])
    half, half_u, half_a = units // 2, width // 2, cols // 2

    bias_sums = sum(part[2] for part in attn_parts)
    unit_sums = sum(part[4] for part in ffn_parts)
    row_sums = sum(part[5] for part in ffn_parts)[:6].reshape(1, 1, -1)
    small = jnp.concatenate([bias_sums, unit_sums, jnp.broadcast_to(row_sums, (4, 1, 6 * width))], axis=2)
    small = jnp.stack([small[0], small[2]]) + near(jnp.stack([small[1], small[3]]))
    count_of = {"d": 2, "u": 2, "a": 2, "p": 1, "s": 1}
    helds = {"d": held_d, "u": held_u, "s": small}
    sent = {"d": over_y(held_d[1]), "u": over_y(held_u[1]), "s": over_y(small[1])}
    chain = lax.axis_size("dp") == 4
    middle = (lax.axis_index("dp") == 1) | (lax.axis_index("dp") == 2)
    inward, cross, outward = chain_steps(lax.axis_size("dp")) if chain else (None, None, None)
    tok = (attn_parts[-1][0],)
    mine, got, totals = {}, {}, {}
    for step in STEPS:
        what, key = step.split()
        if what == "out":
            terms = {"a": attn_terms, "p": proj_terms}[key]
            share = wgrad(following(terms, *tok), 1)
            got[key] = near(share)
            tok = (share,)
        elif what == "held":
            terms = {"a": attn_terms, "p": proj_terms}[key]
            helds[key] = wgrad(following(terms, *tok), 0, got[key])
            sent[key] = over_y(helds[key][1])
            tok = (helds[key],)
        elif what == "take":
            held = after(helds[key], *tok)
            part = held.shape[1] // count_of[key]
            for i in range(count_of[key]):
                k = key + str(i)
                mine[k] = held[0, i * part:(i + 1) * part] + sent[key][i * part:(i + 1) * part]
                tok = (mine[k],)
                if chain and "in " + k not in STEPS:
                    got[k] = lax.ppermute(mine[k], "dp", inward[0])
                elif not chain:
                    totals[k] = chain_sum(mine[k], "dp")
        elif not chain:
            continue
        elif what == "in":
            got[key] = lax.ppermute(after(mine[key], *tok), "dp", inward[0])
        elif what == "fin":
            totals[key] = jnp.where(middle, after(mine[key], *tok), got[key])
            tok = (totals[key],)
        else:
            mine[key] = after(mine[key], *tok) + got[key]
            tok = (mine[key],)
            got[key] = lax.ppermute(mine[key], "dp", cross if what == "cross" else outward[0])
    small = totals["s0"]
    totals = [totals[k] for k in ("d0", "d1", "u0", "u1", "a0", "a1", "p0")]
    totals = [t.astype(F32) for t in totals]
    small = small[0]
    g_attn = jnp.concatenate(totals[4:6], axis=0).reshape(heads, -1, width).transpose(2, 0, 1)
    bias_sum = small[:cols].reshape(heads, 3, -1)
    grad_attn_bias = jnp.concatenate([bias_sum[:, 0], bias_sum[:, 2]], axis=1)
    rowed = small[cols + units:].reshape(6, 1, width)
    return (
        jnp.concatenate(outputs).reshape(1, micro, rows, width),
        jnp.concatenate([part[0] for part in attn_parts]).reshape(1, micro, rows, width),
        g_attn[None],
        grad_attn_bias[None],
        totals[6].reshape(proj_weight.shape),
        rowed[0],
        rowed[1],
        rowed[2],
        jnp.concatenate(totals[2:4], axis=0)[None],
        small[None, cols:cols + units],
        jnp.concatenate(totals[:2], axis=0)[None],
        rowed[3],
        rowed[4],
        rowed[5],
    )


def solution(mesh):
    rows = P(None, ("dp", "tensor"), None)
    layer = P("section", None)
    placed = (
        rows, rows, P(None, "dp"), P(None, "dp", None),
        P("section", None, "tensor", None), P("section", "tensor", None), P("section", "tensor", None, None),
        layer, layer, layer, P("section", None, "tensor"), P("section", "tensor"), P("section", "tensor", None),
        layer, layer, layer,
    )
    both = P("section", None, ("dp", "tensor"), None)
    return jax.shard_map(
        body,
        mesh=mesh,
        in_specs=placed,
        out_specs=(both, both) + placed[4:],
        check_vma=False,
    )
```

```python
import functools

import jax
import jax.numpy as jnp
from jax import lax
from jax.experimental import pallas as pl
from jax.experimental.pallas import tpu as pltpu
from jax.sharding import PartitionSpec as P

HD = 64
SEQLEN = 208
norm_eps = 1e-06
masked_value = -1000000000.0
BF = jnp.bfloat16
F32 = jnp.float32
NT = (((1,), (1,)), ((), ()))
TN = (((0,), (0,)), ((), ()))
MIB = 1 << 20
PARTS = 3
EXTRA = 32


def dot(a, b):
    return jnp.dot(a, b, preferred_element_type=F32)


def dot_nt(a, b):
    return lax.dot_general(a, b, NT, preferred_element_type=F32)


def dot_tn(a, b):
    return lax.dot_general(a, b, TN, preferred_element_type=F32)


def normed(residual):
    center = residual - jnp.mean(residual, axis=-1, keepdims=True)
    rstd = lax.rsqrt(jnp.mean(center * center, axis=-1, keepdims=True) + norm_eps)
    return center * rstd, rstd


def norm_back(grad, n, rstd, gain):
    g = grad * gain
    return rstd * (g - jnp.mean(g, axis=-1, keepdims=True) - n * jnp.mean(g * n, axis=-1, keepdims=True))


def gelu_parts(u, slope):
    short = u.astype(BF)
    size = jnp.abs(short)
    t = pl.reciprocal(1.0 + 0.23164189 * jnp.abs(u), approx=True).astype(BF)
    terms = [BF(c) for c in (0.127414796, -0.142248368, 0.7107068705, -0.7265760135, 0.5307027145)]
    poly = t * (terms[0] + t * (terms[1] + t * (terms[2] + t * (terms[3] + t * terms[4]))))
    bell = jnp.exp2(u * (u * -0.7213475204444817)).astype(BF)
    tail = poly * bell
    act = jnp.maximum(short, BF(0.0)) - size * tail
    if not slope:
        return act, None
    return act, jnp.where(short < 0, tail, BF(1.0) - tail) + short * (bell * BF(0.3989422804014327))


def fixed(a):
    return pl.BlockSpec(a.shape, lambda q: (0,) * len(a.shape))


def quarter(a):
    return pl.BlockSpec((1,) + tuple(a.shape[1:]), lambda q: (q,) + (0,) * (len(a.shape) - 1))


def call(kernel, name, count, ins, outs, scratch, flops, limit=24):
    spec = lambda pair: (quarter if pair[1] else fixed)(pair[0])
    size = sum(a.size * a.dtype.itemsize for a, _ in (*ins, *outs))
    return pl.pallas_call(
        kernel,
        grid=(count,),
        in_specs=[spec(p) for p in ins],
        out_specs=[spec(p) for p in outs],
        out_shape=[a for a, _ in outs],
        scratch_shapes=scratch,
        compiler_params=pltpu.CompilerParams(vmem_limit_bytes=limit * MIB),
        cost_estimate=pl.CostEstimate(flops=1, bytes_accessed=1, transcendentals=0),
        name=name,
    )(*[a for a, _ in ins])


def shape(*dims, t=BF):
    return jax.ShapeDtypeStruct(dims, t)


def units_of(p, seqs):
    for s in range(seqs):
        for h in range(p.shape[1] // (3 * HD)):
            yield s, h


def head_rows(p, s, h, part):
    at = (3 * h + part) * HD
    return p[s * SEQLEN:(s + 1) * SEQLEN, at:at + HD]


def attn_fwd_kernel(save, first, seqs, x_ref, ok_ref, base_ref, ab_ref, wt_ref, pw_ref, r1_ref, *saved):
    q = pl.program_id(0)
    x = x_ref[...]

    @pl.when(q == 0)
    def _():
        r1_ref[...] = x.astype(F32) + base_ref[...] if first else base_ref[...]

    cols = ab_ref.shape[2]
    p = (dot_nt(x, wt_ref[0, :cols]) + ab_ref[0]).astype(BF)
    blocks = list(units_of(p, seqs))
    oks = [ok_ref[s] > 0 for s in range(seqs)]
    scores = [dot_nt(head_rows(p, s, h, 1), head_rows(p, s, h, 0) * 0.125) for s, h in blocks]
    probs = []
    for (s, h), st in zip(blocks, scores):
        st = jnp.where(oks[s], st, masked_value)
        e = jnp.exp(st - jnp.max(st, axis=0, keepdims=True))
        probs.append((e * (1.0 / jnp.sum(e, axis=0, keepdims=True))).astype(BF))
    cts = [dot_tn(head_rows(p, s, h, 2), a).astype(BF) for (s, h), a in zip(blocks, probs)]
    per = len(blocks) // seqs
    c = jnp.concatenate([jnp.concatenate(cts[s * per:(s + 1) * per], axis=0).T for s in range(seqs)], axis=0)
    r1_ref[...] += dot(c, pw_ref[0])
    if save:
        saved[0][0] = p
        saved[1][0] = c
        for (s, h), a in zip(blocks, probs):
            saved[2][0, s, h] = a


def attn_fwd(x, ok, base, ab, wt, pw, save, first):
    rows, width = x.shape
    count, _, cols = ab.shape
    seqs, heads = rows // SEQLEN, cols // (3 * HD)
    outs = [(shape(rows, width, t=F32), False)]
    if save:
        outs += [(shape(count, rows, cols), True), (shape(count, rows, heads * HD), True),
                 (shape(count, seqs, heads, SEQLEN, SEQLEN), True)]
    flops = count * 2 * rows * (width * cols + heads * HD * (2 * SEQLEN + width))
    ins = [(x, False), (ok, False), (base, False), (ab, True), (wt, True), (pw, True)]
    return call(functools.partial(attn_fwd_kernel, save, first, seqs), "attn_fwd", count, ins, outs, [], flops)


def ffn_fwd_kernel(save, first, last, x_ref, acc_in, vec_ref, ub_ref, up_ref, down_ref, *outs):
    q = pl.program_id(0)
    outs, (hb_ref, acc_ref) = outs[:-2], outs[-2:]

    @pl.when(q == 0)
    def _():
        if first:
            h = normed(x_ref[...])[0] * vec_ref[0:1] + vec_ref[1:2]
            hb_ref[...] = h.astype(BF)
            acc_ref[...] = h + vec_ref[2:3]
        else:
            hb_ref[...] = x_ref[...]
            acc_ref[...] = acc_in[...]

    hb = hb_ref[...]
    units = up_ref.shape[2]
    pieces = 2
    step = units // pieces
    us = [dot(hb, up_ref[0, :, j * step:(j + 1) * step]) for j in range(pieces)]
    es, slopes = [], []
    for j, u in enumerate(us):
        act, slope = gelu_parts(u + ub_ref[0, :, j * step:(j + 1) * step], save)
        es.append(act.astype(BF))
        if save:
            outs[2][0, :, j * step:(j + 1) * step] = slope.astype(BF)
    e = jnp.concatenate(es, axis=1)
    if save:
        outs[1][0] = e
    acc_ref[...] += dot(e, down_ref[0])

    @pl.when(q == pl.num_programs(0) - 1)
    def _():
        acc = acc_ref[...]
        if last:
            outs[0][...] = (normed(acc)[0] * vec_ref[3:4] + vec_ref[4:5]).astype(BF)
            if save:
                outs[3][...] = acc
                outs[4][...] = hb
        else:
            outs[0][...] = acc
            outs[1][...] = hb


def ffn_fwd(x, acc, vec, ub, up, down, save, first, last):
    rows, width = x.shape
    count, _, units = ub.shape
    outs = [(shape(rows, width, t=BF if last else F32), False)]
    if save:
        outs += [(shape(count, rows, units), True)] * 2 + [(shape(rows, width, t=F32), False), (shape(rows, width), False)]
    if not last:
        outs += [(shape(rows, width), False)]
    ins = [(x, False), (acc, False), (vec, False), (ub, True), (up, True), (down, True)]
    scratch = [pltpu.VMEM((rows, width), BF), pltpu.VMEM((rows, width), F32)]
    return call(functools.partial(ffn_fwd_kernel, save, first, last), "ffn_fwd", count, ins, outs, scratch,
                count * 4 * rows * width * units)


def ffn_bwd_kernel(full, dy_ref, r2_ref, r1_ref, vec_ref, slope_ref, up_ref, down_ref, *outs):
    q = pl.program_id(0)
    outs, (df_ref, dh_ref, sum_ref) = outs[:-3], outs[-3:]
    total = lambda v: jnp.sum(v, axis=0, keepdims=True)

    @pl.when(q == 0)
    def _():
        dy = dy_ref[...].astype(F32)
        n2, s2 = normed(r2_ref[...])
        dr2 = norm_back(dy, n2, s2, vec_ref[3:4])
        df_ref[...] = dr2.astype(BF)
        dh_ref[...] = dr2
        if full:
            sum_ref[0:1] = total(dr2)
            sum_ref[1:2] = total(dy * n2)
            sum_ref[2:3] = total(dy)

    df = df_ref[...]
    units = up_ref.shape[2]
    step = units // PARTS
    des = [dot_nt(df, down_ref[0, j * step:(j + 1) * step]) for j in range(PARTS)]
    dus = [(de * slope_ref[0, :, j * step:(j + 1) * step].astype(F32)).astype(BF) for j, de in enumerate(des)]
    du = jnp.concatenate(dus, axis=1)
    dh_ref[...] += dot_nt(du, up_ref[0])
    if full:
        outs[3][0] = du
        outs[4][0] = total(du.astype(F32))

    @pl.when(q == pl.num_programs(0) - 1)
    def _():
        dh = dh_ref[...]
        n1, s1 = normed(r1_ref[...])
        dr1 = norm_back(dh, n1, s1, vec_ref[0:1])
        outs[0][...] = dr1
        outs[1][...] = dr1.astype(BF)
        if full:
            outs[2][...] = df
            outs[5][0:1] = total(dr1)
            outs[5][1:2] = total(dh * n1)
            outs[5][2:3] = total(dh)
            outs[5][3:6] = sum_ref[0:3]
            outs[5][6:8] = jnp.zeros_like(outs[5][6:8])


def ffn_bwd(dy, r2, r1, vec, slope, up, down, full):
    rows, width = r1.shape
    count, _, units = slope.shape
    outs = [(shape(rows, width, t=F32), False), (shape(rows, width), False)]
    if full:
        outs += [(shape(rows, width), False), (shape(count, rows, units), True),
                 (shape(count, 1, units, t=F32), True), (shape(8, width, t=F32), False)]
    ins = [(dy, False), (r2, False), (r1, False), (vec, False), (slope, True), (up, True), (down, True)]
    scratch = [pltpu.VMEM((rows, width), BF), pltpu.VMEM((rows, width), F32), pltpu.VMEM((8, width), F32)]
    return call(functools.partial(ffn_bwd_kernel, full), "ffn_bwd", count, ins, outs, scratch,
                count * 4 * rows * width * units)


def attn_bwd_kernel(full, seqs, dg_ref, dr1_ref, p_ref, a_ref, wt_ref, pw_ref, *outs):
    q = pl.program_id(0)
    outs, dx_ref = outs[:-1], outs[-1]

    @pl.when(q == 0)
    def _():
        dx_ref[...] = dr1_ref[...]

    dc = dot_nt(dg_ref[...], pw_ref[0]).astype(BF)
    p = p_ref[0]
    blocks = list(units_of(p, seqs))
    dcs = [dc[s * SEQLEN:(s + 1) * SEQLEN, h * HD:(h + 1) * HD] for s, h in blocks]
    das = [dot_nt(head_rows(p, s, h, 2), d) for (s, h), d in zip(blocks, dcs)]
    dss = []
    for (s, h), da in zip(blocks, das):
        a = a_ref[0, s, h].astype(F32)
        dss.append((a * (da - jnp.sum(da * a, axis=0, keepdims=True))).astype(BF))
    pieces = []
    for (s, h), d, ds in zip(blocks, dcs, dss):
        dq = dot_tn(ds, head_rows(p, s, h, 1)) * 0.125
        dk = dot(ds, head_rows(p, s, h, 0)) * 0.125
        dv = dot(a_ref[0, s, h], d)
        pieces += [dq.astype(BF), dk.astype(BF), dv.astype(BF)]
    per = len(pieces) // seqs
    dp = jnp.concatenate([jnp.concatenate(pieces[s * per:(s + 1) * per], axis=1) for s in range(seqs)], axis=0)
    dx_ref[...] += dot(dp, wt_ref[0, :dp.shape[1]])
    if full:
        outs[1][0] = dp
        outs[2][0] = jnp.sum(dp.astype(F32), axis=0, keepdims=True)

    @pl.when(q == pl.num_programs(0) - 1)
    def _():
        outs[0][...] = dx_ref[...].astype(outs[0].dtype)


def attn_bwd(dg, dr1, p, a, wt, pw, full):
    rows, width = dg.shape
    count, _, cols = p.shape
    seqs, heads = rows // SEQLEN, cols // (3 * HD)
    outs = [(shape(rows, width, t=F32 if full else BF), False)]
    if full:
        outs += [(shape(count, rows, cols), True), (shape(count, 1, cols, t=F32), True)]
    ins = [(dg, False), (dr1, False), (p, True), (a, True), (wt, True), (pw, True)]
    flops = count * 2 * rows * (width * cols + heads * HD * (4 * SEQLEN + width))
    return call(functools.partial(attn_bwd_kernel, full, seqs), "attn_bwd", count, ins, outs,
                [pltpu.VMEM((rows, width), F32)], flops)


def wgrad_kernel(pairs, *refs):
    total = None
    for g in range(pairs):
        a, b = refs[2 * g], refs[2 * g + 1]
        a = a[0] if len(a.shape) == 3 else a[...]
        b = b[0] if len(b.shape) == 3 else b[...]
        part = dot_tn(a, b)
        total = part if total is None else total + part
    for more in refs[2 * pairs:-1]:
        total = total + more[0].astype(F32)
    refs[-1][0] = total.astype(BF)


def wgrad(pairs, odd, *more):
    def spec(a):
        if a.ndim == 2:
            return pl.BlockSpec(a.shape, lambda i: (0, 0))
        return pl.BlockSpec((1,) + a.shape[1:], lambda i: (2 * i + odd, 0, 0))

    flat = [a for pair in pairs for a in pair]
    dims = (2, pairs[0][0].shape[-1], pairs[0][1].shape[-1])
    block = pl.BlockSpec((1,) + dims[1:], lambda i: (i, 0, 0))
    return pl.pallas_call(
        functools.partial(wgrad_kernel, len(pairs)),
        grid=(2,),
        in_specs=[spec(a) for a in flat] + [block] * len(more),
        out_specs=block,
        out_shape=shape(*dims),
        compiler_params=pltpu.CompilerParams(vmem_limit_bytes=24 * MIB),
        cost_estimate=pl.CostEstimate(flops=1, bytes_accessed=1, transcendentals=0),
        name="wgrad",
    )(*flat, *more)


STEPS = (
    "out a", "out p", "take d", "held a", "held p", "cross d0", "in d1", "cross d1",
    "take u", "outw d0", "cross u0", "in u1", "outw d1", "fin d0", "take a", "cross u1",
    "outw u0", "cross a0", "in a1", "fin d1", "outw u1", "take s", "take p", "cross a1",
    "outw a0", "fin u0", "cross s0", "cross p0", "fin u1", "outw a1", "outw s0", "outw p0",
    "fin a0", "fin a1", "fin s0", "fin p0",
)


def swapped(value, axis, bit):
    count = lax.axis_size(axis)
    return lax.ppermute(value, axis, [(i, i ^ bit) for i in range(count)])


def near(value):
    return swapped(value, "tensor", 1)


def over_y(value):
    return swapped(value, "tensor", 2)


def chain_steps(count):
    half = count // 2
    inward = [[(s, s + 1), (count - 1 - s, count - 2 - s)] for s in range(half - 1)]
    outward = [[(s, s - 1), (count - 1 - s, count - s)] for s in range(half - 1, 0, -1)]
    return inward, [(half - 1, half), (half, half - 1)], outward


def chain_sum(value, axis):
    count = lax.axis_size(axis)
    if count == 1:
        return value
    if count % 2:
        return lax.psum(value, axis)
    here = lax.axis_index(axis)
    inward, cross, outward = chain_steps(count)
    for step in inward:
        value = value + lax.ppermute(value, axis, step)
    value = value + lax.ppermute(value, axis, cross)
    for step in outward:
        got = lax.ppermute(value, axis, step)
        takes = (here == step[0][1]) | (here == step[1][1])
        value = jnp.where(takes, got, value)
    return value


def after(value, *others):
    return lax.optimization_barrier((value, *others))[0]


def key_allowed(region_count, region_mask, caption):
    regions = region_mask.shape[-1]
    slot_index = jnp.arange(caption + regions, dtype=jnp.int32) - caption
    caption_ones = jnp.ones(region_mask.shape[:-1] + (caption,), jnp.int32)
    present = jnp.concatenate([caption_ones, region_mask], axis=-1) > 0
    return present & (slot_index < region_count[..., None])


def three_parts(vector):
    high = lax.reduce_precision(vector, 8, 7)
    mid = lax.reduce_precision(vector - high, 8, 7)
    return [high, mid, vector - high - mid]


def body(
    layer_input, cotangent, region_count, region_mask, attn_weight, attn_bias, proj_weight, proj_bias,
    first_gain, first_shift, up_weight, up_bias, down_weight, down_bias, second_gain, second_shift,
):
    section = lax.axis_index("section")
    tensor = lax.axis_index("tensor")
    micro, rows, width = layer_input.shape
    heads = attn_weight.shape[2]
    cols = heads * attn_weight.shape[3]
    units = up_weight.shape[2]
    assert rows == SEQLEN and lax.axis_size("tensor") == 4
    dp_pairs = lax.axis_size("dp") % 2 == 0
    odd = lax.axis_index("dp") % 2 == 1

    pieces = attn_bias[0].reshape(heads, 2, -1)
    own_bias = jnp.stack([pieces[:, 0], jnp.zeros_like(pieces[:, 0]), pieces[:, 1]], axis=1).reshape(-1)
    own_bias = jnp.pad(own_bias, (0, width - cols))
    tail = jnp.stack(three_parts(own_bias) + three_parts(up_bias[0])).astype(BF)
    tail = after(jnp.pad(tail, ((0, EXTRA - 6), (0, 0))))
    attn_own = attn_weight[0].transpose(1, 2, 0).reshape(cols, width)
    attn_own = jnp.concatenate([attn_own, tail], axis=0)
    proj_own = proj_weight[0].reshape(-1, width)
    up_own = up_weight[0]
    down_own = down_weight[0]

    def part(own):
        half = own.shape[0] // 2
        return jnp.where(odd, own[half:], own[:half]) if dp_pairs else own

    def along_dp(mine):
        return swapped(mine, "dp", 1) if dp_pairs else mine

    def both_halves(mine, pair):
        if not dp_pairs:
            return mine
        return jnp.where(odd, jnp.concatenate([pair, mine]), jnp.concatenate([mine, pair]))

    def pair_of(a, b):
        return jnp.stack([a, b])

    ok = lax.dynamic_index_in_dim(key_allowed(region_count, region_mask, rows - region_mask.shape[-1]), tensor, 1, False)
    ok = ok.astype(jnp.int32)[:, :, None]
    vec = jnp.concatenate([first_gain, first_shift, down_bias, second_gain, second_shift], axis=0)
    groups = 2 if micro % 2 == 0 else 1
    per = micro // groups
    size = per * rows
    cut = lambda value: [value.reshape(micro * rows, -1)[g * size:(g + 1) * size] for g in range(groups)]
    oks = [ok[g * per:(g + 1) * per] for g in range(groups)]
    x_own, cots = cut(layer_input), cut(cotangent)

    attn_mine = over_y(part(attn_own))
    attn_near = near(attn_own)
    proj_mine = over_y(part(proj_own))
    proj_near = near(proj_own)
    up_mine = over_y(after(part(up_own), attn_mine))
    attn_pair = along_dp(attn_mine)
    up_near = near(up_own)
    down_mine = over_y(after(part(down_own), proj_mine))
    proj_pair = along_dp(proj_mine)
    down_near = near(down_own)
    up_pair = along_dp(up_mine)
    down_pair = along_dp(down_mine)

    def biases(stack):
        three = stack[:, cols:cols + 6].astype(F32)
        return jnp.sum(three[:, :3], axis=1, keepdims=True)[:, :, :cols], jnp.sum(three[:, 3:], axis=1, keepdims=True)

    attn_0 = pair_of(attn_own, attn_near)
    proj_0 = pair_of(proj_own, proj_near)
    up_0 = pair_of(up_own, up_near)
    down_0 = pair_of(down_own, down_near)
    ab_0, ub_0 = biases(attn_0)
    r1s = [attn_fwd(x_own[g], oks[g], proj_bias, ab_0, attn_0, proj_0, False, True)[0] for g in range(groups)]
    attn_far = both_halves(attn_mine, attn_pair)
    attn_1 = pair_of(attn_far, near(attn_far))
    proj_far = both_halves(proj_mine, proj_pair)
    proj_1 = pair_of(proj_far, near(proj_far))
    ab_1, ub_1 = biases(attn_1)
    r1s = [attn_fwd(x_own[g], oks[g], r1s[g], ab_1, attn_1, proj_1, False, False)[0] for g in range(groups)]
    halves = [ffn_fwd(r1s[g], vec, vec, ub_0, up_0, down_0, False, True, False) for g in range(groups)]
    up_far = both_halves(up_mine, up_pair)
    up_1 = pair_of(up_far, near(up_far))
    down_far = both_halves(down_mine, down_pair)
    down_1 = pair_of(down_far, near(down_far))
    firsts, hops = [], []
    for g in range(groups):
        tok = firsts[-1:]
        acc, hb = halves[g]
        firsts.append(ffn_fwd(hb, after(acc, *tok), vec, ub_1, up_1, down_1, False, False, True)[0])
        hops.append(swapped(after(firsts[g], *hops[-1:]), "section", 1))

    tok = firsts[-1]
    attn_w = jnp.concatenate([after(attn_0, tok), attn_1])
    proj_w = jnp.concatenate([after(proj_0, tok), proj_1])
    up_w = jnp.concatenate([after(up_0, tok), up_1])
    down_w = jnp.concatenate([after(down_0, tok), down_1])
    ab = jnp.concatenate([ab_0, ab_1])
    ub = jnp.concatenate([ub_0, ub_1])

    kept, outputs, backs = [], [], []
    tok = (up_w, down_w)
    for g in range(groups):
        x = jnp.where(section == 0, after(x_own[g], *tok), hops[g])
        r1, p, c, a = attn_fwd(x, oks[g], proj_bias, ab, attn_w, proj_w, True, True)
        y, e, slope, r2, hb = ffn_fwd(r1, vec, vec, ub, up_w, down_w, True, True, True)
        dr1, dg = ffn_bwd(cots[g], r2, r1, vec, slope, up_w, down_w, False)
        (d_first,) = attn_bwd(dg, dr1, p, a, attn_w, proj_w, False)
        backs.append(swapped(d_first, "section", 1))
        kept.append((x, r1, p, c, a, e, slope, r2, hb))
        outputs.append(y)
        tok = (d_first,)

    def ffn_part(g, *before):
        x, r1, p, c, a, e, slope, r2, hb = kept[g]
        dy = jnp.where(section == 1, after(cots[g], *before), backs[g])
        return ffn_bwd(dy, r2, r1, vec, slope, up_w, down_w, True)

    def attn_part(g, dg, dr1):
        x, r1, p, c, a, e, slope, r2, hb = kept[g]
        return attn_bwd(dg, dr1, p, a, attn_w, proj_w, True)

    ffn_parts, attn_parts = [], []
    down_pre, up_pre = [[], []], [[], []]

    def following(terms, *before):
        return [(after(terms[0][0], *before), terms[0][1])] + terms[1:]

    for g in range(groups):
        ffn_parts.append(ffn_part(g, *tok))
        if g < groups - 1:
            down_term = (kept[g][5], ffn_parts[g][2])
            up_term = (kept[g][8], ffn_parts[g][3])
            for odd_share in (1, 0):
                down_pre[odd_share] = [wgrad([down_term], odd_share, *down_pre[odd_share])]
                up_pre[odd_share] = [wgrad([up_term], odd_share, *up_pre[odd_share])]
            tok = (*down_pre[0], *down_pre[1], *up_pre[0], *up_pre[1])
    g = groups - 1
    down_terms, up_terms = [(kept[g][5], ffn_parts[g][2])], [(kept[g][8], ffn_parts[g][3])]
    all_of = lambda a, b: [(a(g), b(g)) for g in range(groups)]
    proj_terms = all_of(lambda g: kept[g][3], lambda g: ffn_parts[g][1])

    out_d = wgrad(down_terms, 1, *down_pre[1])
    got_d = near(out_d)
    out_u = wgrad(following(up_terms, out_d), 1, *up_pre[1])
    got_u = near(out_u)
    held_d = wgrad(following(down_terms, out_u), 0, *down_pre[0], got_d)
    held_u = wgrad(following(up_terms, held_d), 0, *up_pre[0], got_u)
    tok = (held_u,)
    for g in range(groups):
        attn_parts.append(attn_part(g, after(ffn_parts[g][1], *tok), ffn_parts[g][0]))
        tok = (attn_parts[g][0],)
    attn_terms = all_of(lambda g: attn_parts[g][1], lambda g: kept[g][0])
    half, half_u, half_a = units // 2, width // 2, cols // 2

    bias_sums = sum(part[2] for part in attn_parts)
    unit_sums = sum(part[4] for part in ffn_parts)
    row_sums = sum(part[5] for part in ffn_parts)[:6].reshape(1, 1, -1)
    small = jnp.concatenate([bias_sums, unit_sums, jnp.broadcast_to(row_sums, (4, 1, 6 * width))], axis=2)
    small = jnp.stack([small[0], small[2]]) + near(jnp.stack([small[1], small[3]]))
    count_of = {"d": 2, "u": 2, "a": 2, "p": 1, "s": 1}
    helds = {"d": held_d, "u": held_u, "s": small}
    sent = {"d": over_y(held_d[1]), "u": over_y(held_u[1]), "s": over_y(small[1])}
    chain = lax.axis_size("dp") == 4
    middle = (lax.axis_index("dp") == 1) | (lax.axis_index("dp") == 2)
    inward, cross, outward = chain_steps(lax.axis_size("dp")) if chain else (None, None, None)
    tok = (attn_parts[-1][0],)
    mine, got, totals = {}, {}, {}
    for step in STEPS:
        what, key = step.split()
        if what == "out":
            terms = {"a": attn_terms, "p": proj_terms}[key]
            share = wgrad(following(terms, *tok), 1)
            got[key] = near(share)
            tok = (share,)
        elif what == "held":
            terms = {"a": attn_terms, "p": proj_terms}[key]
            helds[key] = wgrad(following(terms, *tok), 0, got[key])
            sent[key] = over_y(helds[key][1])
            tok = (helds[key],)
        elif what == "take":
            held = after(helds[key], *tok)
            part = held.shape[1] // count_of[key]
            for i in range(count_of[key]):
                k = key + str(i)
                mine[k] = held[0, i * part:(i + 1) * part] + sent[key][i * part:(i + 1) * part]
                tok = (mine[k],)
                if chain and "in " + k not in STEPS:
                    got[k] = lax.ppermute(mine[k], "dp", inward[0])
                elif not chain:
                    totals[k] = chain_sum(mine[k], "dp")
        elif not chain:
            continue
        elif what == "in":
            got[key] = lax.ppermute(after(mine[key], *tok), "dp", inward[0])
        elif what == "fin":
            totals[key] = jnp.where(middle, after(mine[key], *tok), got[key])
            tok = (totals[key],)
        else:
            mine[key] = after(mine[key], *tok) + got[key]
            tok = (mine[key],)
            got[key] = lax.ppermute(mine[key], "dp", cross if what == "cross" else outward[0])
    small = totals["s0"]
    totals = [totals[k] for k in ("d0", "d1", "u0", "u1", "a0", "a1", "p0")]
    totals = [t.astype(F32) for t in totals]
    small = small[0]
    g_attn = jnp.concatenate(totals[4:6], axis=0).reshape(heads, -1, width).transpose(2, 0, 1)
    bias_sum = small[:cols].reshape(heads, 3, -1)
    grad_attn_bias = jnp.concatenate([bias_sum[:, 0], bias_sum[:, 2]], axis=1)
    rowed = small[cols + units:].reshape(6, 1, width)
    return (
        jnp.concatenate(outputs).reshape(1, micro, rows, width),
        jnp.concatenate([part[0] for part in attn_parts]).reshape(1, micro, rows, width),
        g_attn[None],
        grad_attn_bias[None],
        totals[6].reshape(proj_weight.shape),
        rowed[0],
        rowed[1],
        rowed[2],
        jnp.concatenate(totals[2:4], axis=0)[None],
        small[None, cols:cols + units],
        jnp.concatenate(totals[:2], axis=0)[None],
        rowed[3],
        rowed[4],
        rowed[5],
    )


def solution(mesh):
    rows = P(None, ("dp", "tensor"), None)
    layer = P("section", None)
    placed = (
        rows, rows, P(None, "dp"), P(None, "dp", None),
        P("section", None, "tensor", None), P("section", "tensor", None), P("section", "tensor", None, None),
        layer, layer, layer, P("section", None, "tensor"), P("section", "tensor"), P("section", "tensor", None),
        layer, layer, layer,
    )
    both = P("section", None, ("dp", "tensor"), None)
    return jax.shard_map(
        body,
        mesh=mesh,
        in_specs=placed,
        out_specs=(both, both) + placed[4:],
        check_vma=False,
    )
```
